256 devices in a mesh: frame: 32 (over x, z_hi, y), tile: 8 (over z_lo, core).
Axes of the slice: x: 4, y: 4, z: 8 (z_hi: 2, z_lo: 4; z = z_hi * 4 + z_lo), core: 2. Of those that a mesh axis runs over, the one named last changes fastest.
Arguments:
- features: bfloat16 [64, 30720, 256], P('frame', 'tile')
- query_frame: int32 [2048], replicated, may hold values from 0 to 63
- query_row: int32 [2048], replicated, may hold values from 0 to 63
- query_col: int32 [2048], replicated, may hold values from 0 to 479
- conv_weight: float32 [3, 4, 256], replicated, may hold values from -1.75 to 1.75
- conv_bias: float32 [256], replicated, may hold values from -4 to 4
- out_weight: float32 [3, 256], replicated, may hold values from -0.375 to 0.375
Outputs:
- tracks: float32 [64, 3, 2048], P('frame', None, 'tile')
The draws below stay inside these ranges and needn't reach their ends.
All inputs are finite; a program needn't handle non-finite values.
Results may differ from the reference program's by a relative error of at most 0.00035.
Values may be sent and summed in bfloat16 or wider, within the bound.
No kernel may reach another device: no remote copies, remote signals or barrier semaphores. Data moves between devices by JAX's collectives and lax.ppermute only.
A program may use at most 64 MiB of HBM per device.

```python
import math
import jax
import jax.numpy as jnp
import numpy as np
from jax import lax

C = 256
W = 480
Q = 2048
HID = 256
H = 64
FRAMES = 64


def draw_features(key, part):
    key = jax.random.fold_in(key, 11)
    base_key, scale_key = jax.random.split(key)
    base = jax.random.truncated_normal(base_key, -5.0, 5.0, (FRAMES, H * W, C), jnp.float32)
    low, high = (0.5, 2.0)
    unit = jax.random.uniform(scale_key, (FRAMES, H * W, 1), jnp.float32)
    scale = jnp.exp(jnp.log(low) + unit * (jnp.log(high) - jnp.log(low)))
    return (base * scale).astype(jnp.bfloat16)


def plant(values, key, least, largest):
    longest = values.shape.index(max(values.shape))
    spots = []
    for shift in (0, 1):
        where = [jax.random.randint(jax.random.fold_in(key, axis), (), 0, length) for axis, length in enumerate(values.shape)]
        where[longest] = (where[longest] + shift) % values.shape[longest]
        spots.append(tuple(where))
    return values.at[spots[0]].set(least).at[spots[1]].set(largest)


def cumulative_ranks(count, slope):
    loads = [(1 << 20) // math.isqrt(standing ** slope) + 1 for standing in range(1, count + 1)]
    spread = 1 + sum(loads) // (1 << 30)
    return np.cumsum(np.array([max(1, weight // spread) for weight in loads]))


def skewed_ids(key, extent, amount, lean):
    grid = cumulative_ranks(amount, lean)
    pick = jax.random.randint(jax.random.fold_in(key, 1), extent, 0, int(grid[amount - 1]))
    rank = jnp.searchsorted(jnp.asarray(grid, jnp.int32), pick, side="right")
    return jax.random.permutation(jax.random.fold_in(key, 2), amount)[rank].astype(jnp.int32)


def centred(stream_key, dims, width, limit, held_as=jnp.bfloat16):
    array = jax.random.normal(stream_key, dims, jnp.float32) * width
    return jnp.minimum(jnp.maximum(array, -limit), limit).astype(held_as)


def setup_inputs(seed: int = 0) -> dict:
    streams_of = jax.random.split(jax.random.key(seed), 8)
    features = draw_features(jax.random.fold_in(streams_of[7], 71), 0)
    query_frame = plant(skewed_ids(streams_of[1], (Q,), FRAMES, 2), jax.random.fold_in(streams_of[1], 3), 0, FRAMES - 1).astype(jnp.int32)
    query_row = plant(jax.random.randint(streams_of[2], (Q,), 0, H), jax.random.fold_in(streams_of[2], 1), 0, H - 1).astype(jnp.int32)
    query_col = plant(jax.random.randint(streams_of[3], (Q,), 0, W), jax.random.fold_in(streams_of[3], 1), 0, W - 1).astype(jnp.int32)
    conv_weight = centred(streams_of[4], (3, 4, HID), 12 ** -0.5, 1.75, jnp.float32)
    conv_bias = centred(streams_of[5], (HID,), 1.0, 4.0, jnp.float32)
    out_weight = centred(streams_of[6], (3, HID), HID ** -0.5, 0.375, jnp.float32)
    return dict(features=features, query_frame=query_frame, query_row=query_row, query_col=query_col, conv_weight=conv_weight, conv_bias=conv_bias, out_weight=out_weight)


def reference(features, query_frame, query_row, query_col, conv_weight, conv_bias, out_weight):
    flat = query_row.astype(jnp.int32) * W + query_col.astype(jnp.int32)
    query_feat = features[query_frame.astype(jnp.int32), flat]
    query_wide = query_feat.astype(jnp.float32)
    pixels = jnp.arange(H * W)
    coord_x = (pixels % W).astype(jnp.float32) / W
    coord_y = (pixels // W).astype(jnp.float32) / H

    def one_frame(frame_feat):
        scores = jnp.dot(query_wide, frame_feat.astype(jnp.float32).T, precision=lax.Precision.HIGHEST) / 16.0
        peak = jnp.max(scores, axis=1)
        expo = jnp.exp(scores - peak[:, None])
        total = jnp.sum(expo, axis=1)
        pos_x = jnp.sum(expo * coord_x[None, :], axis=1) / total
        pos_y = jnp.sum(expo * coord_y[None, :], axis=1) / total
        return jnp.stack([pos_x, pos_y, -jnp.log(total), peak + jnp.log(total) - math.log(H * W)])

    inputs = lax.map(one_frame, features)
    padded = jnp.pad(inputs, ((1, 1), (0, 0), (0, 0)))
    count = inputs.shape[0]
    acc = conv_bias[None, :, None]
    for k in range(3):
        acc = acc + jnp.einsum("tcq,ch->thq", padded[k:k + count], conv_weight[k], precision=lax.Precision.HIGHEST)
    hidden = jax.nn.gelu(acc)
    delta = jnp.einsum("thq,oh->toq", hidden, out_weight, precision=lax.Precision.HIGHEST)
    return inputs[:, 0:3] + delta
```

```python
import functools
import math

import jax
import jax.numpy as jnp
from jax import lax
from jax.experimental import pallas as pl
from jax.experimental.pallas import tpu as pltpu
from jax.sharding import PartitionSpec as P

W = 480
LOG2E = math.log2(math.e)
HIGHEST = lax.Precision.HIGHEST
BOTH = ("frame", "tile")


def mesh_groups():
    plane = [[x * 8 + zh * 4 + y for x in range(4) for y in range(4)] for zh in range(2)]
    column = [
        [(x * 8 + zh * 4 + y) * 8 + zl * 2 + c for zh in range(2) for zl in range(4)]
        for x in range(4)
        for y in range(4)
        for c in range(2)
    ]
    return plane, column


def pick_kernel(rows_here, qf_ref, qr_ref, qc_ref, feat_ref, keep_ref, send_ref, vm, sm, slots, sem_m, sem):
    frame_idx, tile_idx = lax.axis_index("frame"), lax.axis_index("tile")
    core = tile_idx % 2
    pix_count = rows_here * W
    frame_count = feat_ref.shape[0] // pix_count
    half = keep_ref.shape[0]
    groups = qf_ref.shape[1]
    frame = qf_ref[...] - frame_idx * frame_count
    row = qr_ref[...] - tile_idx * rows_here
    owned = (frame >= 0) & (frame < frame_count) & (row >= 0) & (row < rows_here)
    sets = qf_ref.shape[0]
    vm[0:sets, :] = frame * pix_count + row * W + qc_ref[...]
    bit = lax.broadcasted_iota(jnp.int32, owned.shape, 0)
    word = jnp.sum(jnp.where(owned, jnp.left_shift(1, bit), 0), axis=0, keepdims=True)
    vm[sets : sets + 8, :] = jnp.broadcast_to(word, (8, groups))
    to_scalar = pltpu.make_async_copy(vm, sm, sem_m)
    to_scalar.start()
    keep_ref[...] = jnp.zeros_like(keep_ref)
    send_ref[...] = jnp.zeros_like(send_ref)
    to_scalar.wait()

    def each(visit, count):
        def group(g, count):
            def more(state):
                return state[0] != 0

            def step(state):
                left, count = state
                low = left & -left
                visit((31 - lax.clz(low)) * groups + g, sm[31 - lax.clz(low), g])
                return left & (left - 1), count + 1

            return lax.while_loop(more, step, (sm[sets, g], count))[1]

        return lax.fori_loop(0, groups, group, count)

    def copy(j, pix):
        first = pl.multiple_of((pix // 16) * 16, 16)
        return pltpu.make_async_copy(feat_ref.at[pl.ds(first, 16), :], slots.at[j], sem)

    found = each(lambda j, pix: copy(j, pix).start(), 0)

    def wait(k, carry):
        copy(0, 0).wait()
        return carry

    lax.fori_loop(0, found, wait, 0)
    sub = lax.broadcasted_iota(jnp.int32, (16, feat_ref.shape[1]), 0)

    def place(j, pix):
        block = slots[j].astype(jnp.float32)
        line = jnp.sum(jnp.where(sub == pix % 16, block, 0.0), axis=0, keepdims=True) * 0.0625
        spot = j % half
        at = pl.ds(pl.multiple_of((spot // 16) * 16, 16), 16)

        def put(ref):
            now = ref[at, :].astype(jnp.float32)
            ref[at, :] = jnp.where(sub == spot % 16, line, now).astype(ref.dtype)

        @pl.when(j // half == core)
        def _():
            put(keep_ref)

        @pl.when(j // half != core)
        def _():
            put(send_ref)

    each(place, 0)


def pick(features, query_frame, query_row, query_col, rows_here):
    flat = features.reshape(-1, features.shape[2])
    queries, chan = query_frame.shape[0], features.shape[2]
    lanes = 128
    sets = queries // lanes
    half = jax.ShapeDtypeStruct((queries // 2, chan), features.dtype)
    vmem = pl.BlockSpec(memory_space=pltpu.VMEM)
    return pl.pallas_call(
        functools.partial(pick_kernel, rows_here),
        out_shape=(half, half),
        in_specs=[vmem, vmem, vmem, pl.BlockSpec(memory_space=pl.ANY)],
        out_specs=(vmem, vmem),
        scratch_shapes=[
            pltpu.VMEM((sets + 8, lanes), jnp.int32),
            pltpu.SMEM((sets + 8, lanes), jnp.int32),
            pltpu.VMEM((queries, 16, chan), features.dtype),
            pltpu.SemaphoreType.DMA,
            pltpu.SemaphoreType.DMA,
        ],
        compiler_params=pltpu.CompilerParams(vmem_limit_bytes=40 << 20),
        name="pick",
    )(*[a.reshape(sets, lanes) for a in (query_frame, query_row, query_col)], flat)


BLOCK = 256
PARTS = 5


def score_kernel(rows_here, own_ref, other_ref, feat_ref, out_ref, fbuf, qbuf, s_ref, sems):
    tile_idx = lax.axis_index("tile")
    core = tile_idx % 2
    frames, pix_count = fbuf.shape[0], fbuf.shape[1]
    copies = [pltpu.make_async_copy(feat_ref.at[f], fbuf.at[f], sems.at[f]) for f in range(frames)]
    for c in copies:
        c.start()
    half_blocks = own_ref.shape[0] // BLOCK
    blocks = 2 * half_blocks
    for b in range(half_blocks):
        qbuf[b] = own_ref[b * BLOCK : (b + 1) * BLOCK, :]
        qbuf[half_blocks + b] = other_ref[b * BLOCK : (b + 1) * BLOCK, :]
    steps = frames * blocks
    span = pix_count // PARTS
    cols = W // PARTS
    total_rows = float(rows_here * lax.axis_size("tile"))
    sub = lax.broadcasted_iota(jnp.int32, (8, BLOCK), 0).astype(jnp.float32)
    zero = jnp.zeros((8, BLOCK), jnp.float32)
    low = jnp.full((8, BLOCK), -jnp.inf, jnp.float32)

    def matmul_part(step, part, top):
        at = pl.ds(pl.multiple_of(part * span, span), span)
        scores = lax.dot_general(
            fbuf[step // blocks, at, :],
            qbuf[step % blocks],
            (((1,), (1,)), ((), ())),
            preferred_element_type=jnp.float32,
        )
        s_ref[step % 2, at, :] = scores
        return jnp.maximum(top, jnp.max(scores.reshape(span // 8, 8, BLOCK), axis=0))

    def sum_part(step, part, peak, sums):
        total, sum_x, sum_y = sums
        for k in range(cols // 8):
            col = part * cols + k * 8
            tail, below = None, None
            for r in reversed(range(rows_here)):
                at = pl.ds(pl.multiple_of(r * W + col, 8), 8)
                expo = jnp.exp2((s_ref[step % 2, at, :] - peak) * LOG2E)
                tail = expo if tail is None else tail + expo
                if r > 0:
                    below = tail if below is None else below + tail
            total = total + tail
            sum_y = sum_y + below
            sum_x = sum_x + tail * (sub + jnp.asarray(col).astype(jnp.float32))
        return total, sum_x, sum_y

    def finish(step, peak, sums):
        total, sum_x, sum_y = [jnp.sum(a, axis=0, keepdims=True) for a in sums]
        first_row = (tile_idx * rows_here).astype(jnp.float32)
        b = step % blocks
        where_to = lax.rem(b + core * half_blocks, blocks)
        packed = jnp.concatenate(
            [peak[0:1], total, sum_x * (1.0 / W), (sum_y + first_row * total) * (1.0 / total_rows)], axis=0
        )
        out_ref[where_to, step // blocks] = packed

    def settle(top):
        return jnp.broadcast_to(jnp.max(top, axis=0, keepdims=True), top.shape)

    copies[0].wait()
    peak = settle(lax.fori_loop(0, PARTS, lambda i, t: matmul_part(0, i, t), low))

    def both(step, peak):
        @pl.when(step % blocks == 0)
        def _():
            for f in range(1, frames):
                @pl.when(step // blocks == f)
                def _():
                    copies[f].wait()

        def part(i, state):
            top, sums = state
            return matmul_part(step, i, top), sum_part(step - 1, i, peak, sums)

        top, sums = lax.fori_loop(0, PARTS, part, (low, (zero, zero, zero)))
        finish(step - 1, peak, sums)
        return settle(top)

    peak = lax.fori_loop(1, steps, both, peak)
    sums = lax.fori_loop(0, PARTS, lambda i, s: sum_part(steps - 1, i, peak, s), (zero, zero, zero))
    finish(steps - 1, peak, sums)


def score(own, other, features, rows_here):
    frames, pix_count, chan = features.shape
    blocks = 2 * own.shape[0] // BLOCK
    vmem = pl.BlockSpec(memory_space=pltpu.VMEM)
    return pl.pallas_call(
        functools.partial(score_kernel, rows_here),
        out_shape=jax.ShapeDtypeStruct((blocks, frames, 4, BLOCK), jnp.float32),
        in_specs=[vmem, vmem, pl.BlockSpec(memory_space=pl.ANY)],
        out_specs=vmem,
        scratch_shapes=[
            pltpu.VMEM((frames, pix_count, chan), features.dtype),
            pltpu.VMEM((blocks, BLOCK, chan), features.dtype),
            pltpu.VMEM((2, pix_count, BLOCK), jnp.float32),
            pltpu.SemaphoreType.DMA((frames,)),
        ],
        compiler_params=pltpu.CompilerParams(vmem_limit_bytes=40 << 20),
        name="score",
    )(own, other, features)


def merge_kernel(pixels, parts_ref, inputs_ref, first_ref, last_ref):
    tiles, frames = parts_ref.shape[0], parts_ref.shape[1]
    for f in range(frames):
        parts = [parts_ref[k, f] for k in range(tiles)]
        peak = functools.reduce(jnp.maximum, [p[0:1] for p in parts])
        sums = functools.reduce(jnp.add, [p[1:4] * jnp.exp(p[0:1] - peak) for p in parts])
        total = sums[0:1]
        log_total = jnp.log(total)
        here = jnp.concatenate(
            [sums[1:2] / total, sums[2:3] / total, -log_total, peak + log_total - math.log(pixels)], axis=0
        )
        inputs_ref[f] = here
        if f == 0:
            first_ref[...] = here
        if f == frames - 1:
            last_ref[...] = here


def merge(parts, pixels):
    tiles, frames, stats, share = parts.shape
    vmem = pl.BlockSpec(memory_space=pltpu.VMEM)
    edge = jax.ShapeDtypeStruct((stats, share), jnp.float32)
    return pl.pallas_call(
        functools.partial(merge_kernel, pixels),
        out_shape=(jax.ShapeDtypeStruct((frames, stats, share), jnp.float32), edge, edge),
        in_specs=[vmem],
        out_specs=(vmem, vmem, vmem),
        name="merge",
    )(parts)


def refine_kernel(before_ref, inputs_ref, after_ref, weight_ref, bias_ref, out_weight_ref, out_ref):
    frames, share = inputs_ref.shape[0], inputs_ref.shape[2]
    bias = jnp.transpose(jnp.broadcast_to(bias_ref[...], (share, bias_ref.shape[1])))
    line = [before_ref[...]] + [inputs_ref[f] for f in range(frames)] + [after_ref[...]]
    for f in range(frames):
        acc = bias
        for k in range(3):
            acc = acc + lax.dot_general(
                weight_ref[k],
                line[f + k],
                (((0,), (0,)), ((), ())),
                precision=HIGHEST,
                preferred_element_type=jnp.float32,
            )
        hidden = jax.nn.gelu(acc)
        delta = jnp.dot(out_weight_ref[...], hidden, precision=HIGHEST, preferred_element_type=jnp.float32)
        out_ref[f] = line[f + 1][0:3] + delta


def refine(before, inputs, after, conv_weight, conv_bias, out_weight):
    frames, _, share = inputs.shape
    return pl.pallas_call(
        refine_kernel,
        out_shape=jax.ShapeDtypeStruct((frames, 3, share), jnp.float32),
        in_specs=[pl.BlockSpec(memory_space=pltpu.VMEM)] * 6,
        out_specs=pl.BlockSpec(memory_space=pltpu.VMEM),
        name="refine",
    )(before, inputs, after, conv_weight, conv_bias[None, :], out_weight)


def local(features, query_frame, query_row, query_col, conv_weight, conv_bias, out_weight):
    frame_count, pix_count, chan = features.shape
    rows_here = pix_count // W
    tiles, groups = lax.axis_size("tile"), lax.axis_size("frame")
    plane, column = mesh_groups()
    keep, send = pick(features, query_frame, query_row, query_col, rows_here)
    swap = [(i, i ^ 1) for i in range(tiles)]
    mine = keep + lax.ppermute(send, "tile", swap)
    wide, tall = len(plane[0]), len(column[0])
    rows = mine.shape[0] // wide
    got = lax.all_to_all(mine.reshape(wide, rows, chan), "frame", 0, 0, axis_index_groups=plane)
    piece = jnp.sum(got, axis=0)
    got = lax.all_to_all(jnp.broadcast_to(piece, (tall, rows, chan)), BOTH, 0, 0, axis_index_groups=column)
    piece = jnp.sum(got, axis=0)
    got = lax.all_to_all(jnp.broadcast_to(piece, (wide, rows, chan)), "frame", 0, 0, axis_index_groups=plane)
    own = got.reshape(wide * rows, chan)
    other = lax.ppermute(own, "tile", swap)
    parts = score(own, other, features, rows_here)
    parts = lax.all_to_all(parts, "tile", 0, 0)
    inputs, first, last = merge(parts, rows_here * tiles * W)
    up = [(i, i + 1) for i in range(groups - 1)]
    before = lax.ppermute(last, "frame", up)
    after = lax.ppermute(first, "frame", [(j, i) for i, j in up])
    return refine(before, inputs, after, conv_weight, conv_bias, out_weight)


def solution(mesh):
    in_specs = (P("frame", "tile", None), P(), P(), P(), P(), P(), P())
    out_specs = P("frame", None, "tile")
    return jax.shard_map(local, mesh=mesh, in_specs=in_specs, out_specs=out_specs, check_vma=False)
```

```python
import functools
import math

import jax
import jax.numpy as jnp
from jax import lax
from jax.experimental import pallas as pl
from jax.experimental.pallas import tpu as pltpu
from jax.sharding import PartitionSpec as P

W = 480
LOG2E = math.log2(math.e)
BOTH = ("frame", "tile")


def mesh_groups():
    plane = [[x * 8 + zh * 4 + y for x in range(4) for y in range(4)] for zh in range(2)]
    column = [
        [(x * 8 + zh * 4 + y) * 8 + zl * 2 + c for zh in range(2) for zl in range(4)]
        for x in range(4)
        for y in range(4)
        for c in range(2)
    ]
    return plane, column


def pick_kernel(rows_here, qf_ref, qr_ref, qc_ref, feat_ref, keep_ref, send_ref, idx, vm, sm, found_at, slots, wide, lines, sems, sem):
    frame_idx, tile_idx = lax.axis_index("frame"), lax.axis_index("tile")
    core = tile_idx % 2
    loads = [
        pltpu.make_async_copy(ref, idx.at[k], sems.at[k]) for k, ref in enumerate((qf_ref, qr_ref, qc_ref))
    ]
    for load in loads:
        load.start()
    pix_count = rows_here * W
    frame_count = feat_ref.shape[0] // pix_count
    half = keep_ref.shape[0]
    sets, groups = idx.shape[1], idx.shape[2]
    lines[...] = jnp.zeros_like(lines)
    for load in loads:
        load.wait()
    frame = idx[0] - frame_idx * frame_count
    row = idx[1] - tile_idx * rows_here
    owned = (frame >= 0) & (frame < frame_count) & (row >= 0) & (row < rows_here)
    vm[0:sets, :] = frame * pix_count + row * W + idx[2]
    bit = lax.broadcasted_iota(jnp.int32, owned.shape, 0)
    word = jnp.sum(jnp.where(owned, jnp.left_shift(1, bit), 0), axis=0, keepdims=True)
    vm[sets : sets + 8, :] = jnp.broadcast_to(word, (8, groups))
    to_scalar = pltpu.make_async_copy(vm, sm, sems.at[3])
    to_scalar.start()
    to_scalar.wait()

    def copy(k, pix):
        first = pl.multiple_of((pix // 16) * 16, 16)
        return pltpu.make_async_copy(feat_ref.at[pl.ds(first, 16), :], slots.at[k], sem)

    def group(g, count):
        def step(state):
            left, count = state
            i = 31 - lax.clz(left & -left)
            pix = sm[i, g]
            copy(count, pix).start()
            found_at[0, count] = i * groups + g
            found_at[1, count] = pix % 16
            return left & (left - 1), count + 1

        return lax.while_loop(lambda state: state[0] != 0, step, (sm[sets, g], count))[1]

    found = lax.fori_loop(0, groups, group, 0)

    def wait(k, carry):
        copy(0, 0).wait()
        return carry

    lax.fori_loop(0, found, wait, 0)

    def place(k, carry):
        wide[k % 8] = slots[k].astype(jnp.float32)
        lines[pl.ds(found_at[0, k], 1), :] = wide[k % 8, pl.ds(found_at[1, k], 1), :]
        return carry

    lax.fori_loop(0, found, place, 0)
    mine = pl.multiple_of(core * half, half)
    theirs = pl.multiple_of((1 - core) * half, half)
    keep_ref[...] = (lines[pl.ds(mine, half), :] * 0.0625).astype(keep_ref.dtype)
    send_ref[...] = (lines[pl.ds(theirs, half), :] * 0.0625).astype(send_ref.dtype)


def pick(features, query_frame, query_row, query_col, rows_here):
    flat = features.reshape(-1, features.shape[2])
    queries, chan = query_frame.shape[0], features.shape[2]
    lanes = 128
    sets = queries // lanes
    half = jax.ShapeDtypeStruct((queries // 2, chan), features.dtype)
    vmem = pl.BlockSpec(memory_space=pltpu.VMEM)
    hbm = pl.BlockSpec(memory_space=pltpu.MemorySpace.HBM)
    return pl.pallas_call(
        functools.partial(pick_kernel, rows_here),
        out_shape=(half, half),
        in_specs=[hbm, hbm, hbm, hbm],
        out_specs=(vmem, vmem),
        scratch_shapes=[
            pltpu.VMEM((3, sets, lanes), jnp.int32),
            pltpu.VMEM((sets + 8, lanes), jnp.int32),
            pltpu.SMEM((sets + 8, lanes), jnp.int32),
            pltpu.SMEM((2, queries), jnp.int32),
            pltpu.VMEM((queries, 16, chan), features.dtype),
            pltpu.VMEM((8, 16, chan), jnp.float32),
            pltpu.VMEM((queries, chan), jnp.float32),
            pltpu.SemaphoreType.DMA((4,)),
            pltpu.SemaphoreType.DMA,
        ],
        compiler_params=pltpu.CompilerParams(vmem_limit_bytes=28 << 20),
        name="pick",
    )(*[a.reshape(sets, lanes) for a in (query_frame, query_row, query_col)], flat)


BLOCK = 256
PARTS = 5
UNITS = 2


def score_kernel(own_ref, other_ref, feat_ref, out_ref, fbuf, even, odd, sems):
    tile_idx = lax.axis_index("tile")
    core = tile_idx % 2
    frames, rows_here = fbuf.shape[0], fbuf.shape[1]
    cols = W // PARTS
    loads = [
        [
            pltpu.make_async_copy(
                feat_ref.at[f, :, pl.ds(i * cols, cols), :], fbuf.at[f, :, pl.ds(i * cols, cols), :], sems.at[f, i]
            )
            for i in range(PARTS)
        ]
        for f in range(frames)
    ]
    for load in loads[0] + loads[1]:
        load.start()
    half_blocks = own_ref.shape[0] // BLOCK
    blocks = 2 * half_blocks
    pairs = blocks // UNITS
    steps = frames * pairs
    total_rows = float(rows_here * lax.axis_size("tile"))
    first_row = (tile_idx * rows_here).astype(jnp.float32)
    sub = lax.broadcasted_iota(jnp.int32, (8, BLOCK), 0).astype(jnp.float32)
    zero = jnp.zeros((8, BLOCK), jnp.float32)
    low = jnp.full((8, BLOCK), -jnp.inf, jnp.float32)

    def stage(pair):
        for m in range(UNITS):
            ref, k = (own_ref, pair * UNITS + m) if pair * UNITS < half_blocks else (other_ref, pair * UNITS + m - half_blocks)
            pltpu.matmul_push_rhs(ref[k * BLOCK : (k + 1) * BLOCK, :], 0, m, transpose=True)

    def run(*accs):
        def feed(f, part, staged):
            for r in range(rows_here):
                lhs = fbuf[f, r, pl.ds(pl.multiple_of(part * cols, 16), cols), :]
                for m in range(UNITS):
                    pltpu.matmul_acc_lhs(accs[m * rows_here + r], lhs, load_staged_rhs=staged if r == 0 else None)

        def drain(kept, part, tops):
            tops = list(tops)
            for r in range(rows_here):
                for m in range(UNITS):
                    scores = pltpu.matmul_pop(accs[m * rows_here + r])
                    kept[part, m, r * cols : (r + 1) * cols, :] = scores
                    tops[m] = jnp.maximum(tops[m], jnp.max(scores.reshape(cols // 8, 8, BLOCK), axis=0))
            return tuple(tops)

        def weigh(kept, part, peaks, sums):
            out = []
            start = jnp.asarray(part * cols).astype(jnp.float32)
            for m in range(UNITS):
                total, sum_x, sum_y = sums[m]
                here, across = None, None
                for k in range(cols // 8):
                    tail, below = None, None
                    for r in reversed(range(rows_here)):
                        at = r * cols + k * 8
                        expo = jnp.exp2((kept[part, m, at : at + 8, :] - peaks[m]) * LOG2E)
                        tail = expo if tail is None else tail + expo
                        if r > 0:
                            below = tail if below is None else below + tail
                    sum_y = sum_y + below
                    here = tail if here is None else here + tail
                    if k > 0:
                        shifted = tail * float(k * 8)
                        across = shifted if across is None else across + shifted
                out.append((total + here, sum_x + (across + here * (sub + start)), sum_y))
            return tuple(out)

        def settle(tops):
            return tuple(jnp.broadcast_to(jnp.max(t, axis=0, keepdims=True), t.shape) for t in tops)

        def finish(step, peaks, sums):
            f, pair = divmod(step, pairs)
            for m in range(UNITS):
                total, sum_x, sum_y = [jnp.sum(a, axis=0, keepdims=True) for a in sums[m]]
                where_to = lax.rem(pair * UNITS + m + core * half_blocks, blocks)
                out_ref[where_to, f] = jnp.concatenate(
                    [peaks[m][0:1], total, sum_x * (1.0 / W), (sum_y + first_row * total) * (1.0 / total_rows)], axis=0
                )

        stage(0)
        peaks = None
        for step in range(steps + 1):
            f = step // pairs
            new, old = (even, odd) if step % 2 == 0 else (odd, even)

            def part_of(i, state, staged=None):
                tops, sums = state
                if step < steps:
                    if step == 0:
                        pltpu.make_async_copy(
                            feat_ref.at[0, :, pl.ds(0, cols), :], fbuf.at[0, :, pl.ds(0, cols), :], sems.at[0, i]
                        ).wait()
                    feed(f, i, staged)
                if step > 0:
                    sums = weigh(old, i, peaks, sums)
                if step < steps:
                    tops = drain(new, i, tops)
                return tops, sums

            if step == pairs:
                for load in loads[1]:
                    load.wait()
            state = ((low,) * UNITS, ((zero, zero, zero),) * UNITS)
            state = part_of(0, state, 0)
            if step + 1 < steps:
                stage((step + 1) % pairs)
            tops, sums = lax.fori_loop(1, PARTS, part_of, state)
            if step > 0:
                finish(step - 1, peaks, sums)
            if step < steps:
                peaks = settle(tops)

    pl.run_scoped(
        run, *[pltpu.ACC(m)((cols, BLOCK), jnp.float32) for m in range(UNITS) for _ in range(rows_here)]
    )


def score(own, other, features, rows_here):
    frames, pix_count, chan = features.shape
    blocks = 2 * own.shape[0] // BLOCK
    vmem = pl.BlockSpec(memory_space=pltpu.VMEM)
    kept = pltpu.VMEM((PARTS, UNITS, pix_count // PARTS, BLOCK), jnp.float32)
    return pl.pallas_call(
        score_kernel,
        out_shape=jax.ShapeDtypeStruct((blocks, frames, 4, BLOCK), jnp.float32),
        in_specs=[vmem, vmem, pl.BlockSpec(memory_space=pltpu.MemorySpace.HBM)],
        out_specs=vmem,
        scratch_shapes=[
            pltpu.VMEM((frames, rows_here, W, chan), features.dtype),
            kept,
            kept,
            pltpu.SemaphoreType.DMA((frames, PARTS)),
        ],
        compiler_params=pltpu.CompilerParams(vmem_limit_bytes=28 << 20),
        name="score",
    )(own, other, features.reshape(frames, rows_here, W, chan))


def merge_kernel(pixels, parts_ref, inputs_ref, first_ref, last_ref):
    tiles, frames = parts_ref.shape[0], parts_ref.shape[1]
    for f in range(frames):
        parts = [parts_ref[k, f] for k in range(tiles)]
        peak = functools.reduce(jnp.maximum, [p[0:1] for p in parts])
        sums = functools.reduce(jnp.add, [p[1:4] * jnp.exp(p[0:1] - peak) for p in parts])
        total = sums[0:1]
        log_total = jnp.log(total)
        here = jnp.concatenate(
            [sums[1:2] / total, sums[2:3] / total, -log_total, peak + log_total - math.log(pixels)], axis=0
        )
        inputs_ref[f] = here
        if f == 0:
            first_ref[...] = here
        if f == frames - 1:
            last_ref[...] = here


def merge(parts, pixels):
    tiles, frames, stats, share = parts.shape
    vmem = pl.BlockSpec(memory_space=pltpu.VMEM)
    edge = jax.ShapeDtypeStruct((stats, share), jnp.float32)
    return pl.pallas_call(
        functools.partial(merge_kernel, pixels),
        out_shape=(jax.ShapeDtypeStruct((frames, stats, share), jnp.float32), edge, edge),
        in_specs=[vmem],
        out_specs=(vmem, vmem, vmem),
        name="merge",
    )(parts)


def split(array, count):
    parts = []
    for _ in range(count):
        parts.append(array.astype(jnp.bfloat16))
        array = array - parts[-1].astype(jnp.float32)
    return parts


MEET = ((0, 0), (0, 1), (1, 0), (1, 1), (0, 2), (2, 0))
DEPTH = 128


def prepare_kernel(weight_ref, bias_ref, out_weight_ref, taps_ref, last_ref):
    taps, stats, hidden = weight_ref.shape
    rows = jnp.concatenate([weight_ref[k] for k in range(taps)] + [jnp.broadcast_to(bias_ref[...], (4, hidden))], axis=0)
    thirds = [p.astype(jnp.float32) for p in split(rows, 3)]
    stacked = jnp.concatenate([thirds[i] for i, _ in MEET], axis=0)
    filler = jnp.zeros((DEPTH - stacked.shape[0], hidden), jnp.float32)
    taps_ref[...] = jnp.transpose(jnp.concatenate([stacked, filler], axis=0)).astype(jnp.bfloat16)
    thirds = [p.astype(jnp.float32) for p in split(out_weight_ref[...], 2)]
    filler = jnp.zeros((8 - out_weight_ref.shape[0], hidden), jnp.float32)
    last_ref[...] = jnp.concatenate([thirds[0], filler, thirds[1], filler], axis=0).astype(jnp.bfloat16)


def prepare(conv_weight, conv_bias, out_weight):
    hidden = conv_bias.shape[0]
    vmem = pl.BlockSpec(memory_space=pltpu.VMEM)
    return pl.pallas_call(
        prepare_kernel,
        out_shape=(
            jax.ShapeDtypeStruct((hidden, DEPTH), jnp.bfloat16),
            jax.ShapeDtypeStruct((16, hidden), jnp.bfloat16),
        ),
        in_specs=[vmem] * 3,
        out_specs=(vmem, vmem),
        cost_estimate=pl.CostEstimate(flops=200000, bytes_accessed=200000, transcendentals=0),
        name="prepare",
    )(conv_weight, conv_bias[None, :], out_weight)


def refine_kernel(before_ref, inputs_ref, after_ref, taps_ref, last_ref, out_ref, held, sem):
    frames, share = inputs_ref.shape[0], inputs_ref.shape[2]
    line = [before_ref[...]] + [inputs_ref[f] for f in range(frames)] + [after_ref[...]]
    unit = jnp.where(lax.broadcasted_iota(jnp.int32, (4, share), 0) == 0, 1.0, 0.0)
    right = []
    for f in range(frames):
        rows = jnp.concatenate([line[f + k] for k in range(3)] + [unit], axis=0)
        thirds = [p.astype(jnp.float32) for p in split(rows, 3)]
        stacked = jnp.concatenate([thirds[j] for _, j in MEET], axis=0)
        filler = jnp.zeros((DEPTH - stacked.shape[0], share), jnp.float32)
        right.append(jnp.concatenate([stacked, filler], axis=0).astype(jnp.bfloat16))
    for f in range(frames):
        acc = jnp.dot(taps_ref[...], right[f], preferred_element_type=jnp.float32)
        hidden = jax.nn.gelu(acc)
        high, rest = split(hidden, 2)
        first = jnp.dot(last_ref[...], high, preferred_element_type=jnp.float32)
        second = jnp.dot(last_ref[...], rest, preferred_element_type=jnp.float32)
        delta = first[0:3] + (first[8:11] + second[0:3])
        held[f] = line[f + 1][0:3] + delta
    store = pltpu.make_async_copy(held, out_ref, sem)
    store.start()
    store.wait()


def refine(before, inputs, after, taps, last):
    frames, _, share = inputs.shape
    return pl.pallas_call(
        refine_kernel,
        out_shape=jax.ShapeDtypeStruct((frames, 3, share), jnp.float32),
        in_specs=[pl.BlockSpec(memory_space=pltpu.VMEM)] * 5,
        out_specs=pl.BlockSpec(memory_space=pltpu.MemorySpace.HBM),
        scratch_shapes=[pltpu.VMEM((frames, 3, share), jnp.float32), pltpu.SemaphoreType.DMA],
        name="refine",
    )(before, inputs, after, taps, last)


def local(features, query_frame, query_row, query_col, conv_weight, conv_bias, out_weight):
    frame_count, pix_count, chan = features.shape
    rows_here = pix_count // W
    tiles, groups = lax.axis_size("tile"), lax.axis_size("frame")
    plane, column = mesh_groups()
    keep, send = pick(features, query_frame, query_row, query_col, rows_here)
    swap = [(i, i ^ 1) for i in range(tiles)]
    mine = keep + lax.ppermute(send, "tile", swap)
    wide, tall = len(plane[0]), len(column[0])
    rows = mine.shape[0] // wide
    got = lax.all_to_all(mine.reshape(wide, rows, chan), "frame", 0, 0, axis_index_groups=plane)
    piece = jnp.sum(got, axis=0)
    got = lax.all_to_all(jnp.broadcast_to(piece, (tall, rows, chan)), BOTH, 0, 0, axis_index_groups=column)
    piece = jnp.sum(got, axis=0)
    got = lax.all_to_all(jnp.broadcast_to(piece, (wide, rows, chan)), "frame", 0, 0, axis_index_groups=plane)
    own = got.reshape(wide * rows, chan)
    other = lax.ppermute(own, "tile", swap)
    parts = score(own, other, features, rows_here)
    parts = lax.all_to_all(parts, "tile", 0, 0)
    inputs, first, last = merge(parts, rows_here * tiles * W)
    up = [(i, i + 1) for i in range(groups - 1)]
    before = lax.ppermute(last, "frame", up)
    after = lax.ppermute(first, "frame", [(j, i) for i, j in up])
    taps, last_weight = prepare(conv_weight, conv_bias, out_weight)
    return refine(before, inputs, after, taps, last_weight)


def solution(mesh):
    in_specs = (P("frame", "tile", None), P(), P(), P(), P(), P(), P())
    out_specs = P("frame", None, "tile")
    return jax.shard_map(local, mesh=mesh, in_specs=in_specs, out_specs=out_specs, check_vma=False)
```

```python
import functools
import math

import jax
import jax.numpy as jnp
from jax import lax
from jax.experimental import pallas as pl
from jax.experimental.pallas import tpu as pltpu
from jax.sharding import PartitionSpec as P

W = 480
LOG2E = math.log2(math.e)
BOTH = ("frame", "tile")


def mesh_groups():
    plane = [[x * 8 + zh * 4 + y for x in range(4) for y in range(4)] for zh in range(2)]
    column = [
        [(x * 8 + zh * 4 + y) * 8 + zl * 2 + c for zh in range(2) for zl in range(4)]
        for x in range(4)
        for y in range(4)
        for c in range(2)
    ]
    return plane, column


BATCH = 4


def pick_kernel(rows_here, qf_ref, qr_ref, qc_ref, feat_ref, keep_ref, send_ref, idx, vm, sm, found_at, slots, wide, lines, sems, sem):
    frame_idx, tile_idx = lax.axis_index("frame"), lax.axis_index("tile")
    core = tile_idx % 2
    loads = [
        pltpu.make_async_copy(ref, idx.at[k], sems.at[k]) for k, ref in enumerate((qf_ref, qr_ref, qc_ref))
    ]
    for load in loads:
        load.start()
    pix_count = rows_here * W
    frame_count = feat_ref.shape[0] // pix_count
    half = keep_ref.shape[0]
    sets, groups = idx.shape[1], idx.shape[2]
    lines[...] = jnp.zeros_like(lines)
    for load in loads:
        load.wait()
    frame = idx[0] - frame_idx * frame_count
    row = idx[1] - tile_idx * rows_here
    owned = (frame >= 0) & (frame < frame_count) & (row >= 0) & (row < rows_here)
    vm[0:sets, :] = frame * pix_count + row * W + idx[2]
    bit = lax.broadcasted_iota(jnp.int32, owned.shape, 0)
    word = jnp.sum(jnp.where(owned, jnp.left_shift(1, bit), 0), axis=0, keepdims=True)
    word = word | jnp.left_shift(pltpu.roll(word, groups // 2, axis=1), sets)
    vm[sets : sets + 8, :] = jnp.broadcast_to(word, (8, groups))
    to_scalar = pltpu.make_async_copy(vm, sm, sems.at[3])
    to_scalar.start()
    to_scalar.wait()

    def copy(k, pix):
        first = pl.multiple_of((pix // 16) * 16, 16)
        return pltpu.make_async_copy(feat_ref.at[pl.ds(first, 16), :], slots.at[k], sem)

    def group(g, count):
        def step(state):
            left, count = state
            i = 31 - lax.clz(left & -left)
            at, lane = i % sets, g + (i // sets) * (groups // 2)
            pix = sm[at, lane]
            copy(count, pix).start()
            found_at[0, count] = at * groups + lane
            found_at[1, count] = pix % 16
            return left & (left - 1), count + 1

        return lax.while_loop(lambda state: state[0] != 0, step, (sm[sets, g], count))[1]

    found = lax.fori_loop(0, groups // 2, group, 0)
    for k in range(BATCH - 1):
        found_at[0, found + k] = lines.shape[0] - 8
        found_at[1, found + k] = 0

    def wait(k, carry):
        copy(0, 0).wait()
        return carry

    lax.fori_loop(0, found, wait, 0)

    def place(batch, carry):
        for k in range(BATCH):
            wide[k] = slots[batch * BATCH + k].astype(jnp.float32)
        picked = [wide[k, pl.ds(found_at[1, batch * BATCH + k], 1), :] for k in range(BATCH)]
        for k in range(BATCH):
            lines[pl.ds(found_at[0, batch * BATCH + k], 1), :] = picked[k]
        return carry

    lax.fori_loop(0, (found + BATCH - 1) // BATCH, place, 0)
    mine = pl.multiple_of(core * half, half)
    theirs = pl.multiple_of((1 - core) * half, half)
    keep_ref[...] = (lines[pl.ds(mine, half), :] * 0.0625).astype(keep_ref.dtype)
    send_ref[...] = (lines[pl.ds(theirs, half), :] * 0.0625).astype(send_ref.dtype)


def pick(features, query_frame, query_row, query_col, rows_here):
    flat = features.reshape(-1, features.shape[2])
    queries, chan = query_frame.shape[0], features.shape[2]
    lanes = 128
    sets = queries // lanes
    half = jax.ShapeDtypeStruct((queries // 2, chan), features.dtype)
    vmem = pl.BlockSpec(memory_space=pltpu.VMEM)
    hbm = pl.BlockSpec(memory_space=pltpu.MemorySpace.HBM)
    return pl.pallas_call(
        functools.partial(pick_kernel, rows_here),
        out_shape=(half, half),
        in_specs=[hbm, hbm, hbm, hbm],
        out_specs=(vmem, vmem),
        scratch_shapes=[
            pltpu.VMEM((3, sets, lanes), jnp.int32),
            pltpu.VMEM((sets + 8, lanes), jnp.int32),
            pltpu.SMEM((sets + 8, lanes), jnp.int32),
            pltpu.SMEM((2, queries + BATCH), jnp.int32),
            pltpu.VMEM((queries + BATCH, 16, chan), features.dtype),
            pltpu.VMEM((BATCH, 16, chan), jnp.float32),
            pltpu.VMEM((queries + 8, chan), jnp.float32),
            pltpu.SemaphoreType.DMA((4,)),
            pltpu.SemaphoreType.DMA,
        ],
        compiler_params=pltpu.CompilerParams(vmem_limit_bytes=56 << 20),
        name="pick",
    )(*[a.reshape(sets, lanes) for a in (query_frame, query_row, query_col)], flat)


BLOCK = 256
PARTS = 5
UNITS = 2


def score_kernel(own_ref, other_ref, feat_ref, out_ref, fbuf, even, odd, sems):
    tile_idx = lax.axis_index("tile")
    core = tile_idx % 2
    frames, rows_here = fbuf.shape[0], fbuf.shape[1]
    cols = W // PARTS
    loads = [
        [
            pltpu.make_async_copy(
                feat_ref.at[f, :, pl.ds(i * cols, cols), :], fbuf.at[f, :, pl.ds(i * cols, cols), :], sems.at[f, i]
            )
            for i in range(PARTS)
        ]
        for f in range(frames)
    ]
    for load in loads[0] + loads[1]:
        load.start()
    half_blocks = own_ref.shape[0] // BLOCK
    blocks = 2 * half_blocks
    pairs = blocks // UNITS
    steps = frames * pairs
    total_rows = float(rows_here * lax.axis_size("tile"))
    first_row = (tile_idx * rows_here).astype(jnp.float32)
    sub = lax.broadcasted_iota(jnp.int32, (8, BLOCK), 0).astype(jnp.float32)
    zero = jnp.zeros((8, BLOCK), jnp.float32)
    low = jnp.full((8, BLOCK), -jnp.inf, jnp.float32)

    def stage(pair):
        for m in range(UNITS):
            ref, k = (own_ref, pair * UNITS + m) if pair * UNITS < half_blocks else (other_ref, pair * UNITS + m - half_blocks)
            pltpu.matmul_push_rhs(ref[k * BLOCK : (k + 1) * BLOCK, :], 0, m, transpose=True)

    def run(*accs):
        def feed(f, part, staged):
            for r in range(rows_here):
                lhs = fbuf[f, r, pl.ds(pl.multiple_of(part * cols, 16), cols), :]
                for m in range(UNITS):
                    pltpu.matmul_acc_lhs(accs[m * rows_here + r], lhs, load_staged_rhs=staged if r == 0 else None)

        def drain(kept, part, tops):
            tops = list(tops)
            for r in range(rows_here):
                for m in range(UNITS):
                    scores = pltpu.matmul_pop(accs[m * rows_here + r])
                    kept[part, m, r * cols : (r + 1) * cols, :] = scores
                    tops[m] = jnp.maximum(tops[m], jnp.max(scores.reshape(cols // 8, 8, BLOCK), axis=0))
            return tuple(tops)

        def weigh(kept, part, peaks, sums):
            out = []
            start = jnp.asarray(part * cols).astype(jnp.float32)
            for m in range(UNITS):
                total, sum_x, sum_y = sums[m]
                here, across = None, None
                for k in range(cols // 8):
                    tail, below = None, None
                    for r in reversed(range(rows_here)):
                        at = r * cols + k * 8
                        expo = jnp.exp2((kept[part, m, at : at + 8, :] - peaks[m]) * LOG2E)
                        tail = expo if tail is None else tail + expo
                        if r > 0:
                            below = tail if below is None else below + tail
                    sum_y = sum_y + below
                    here = tail if here is None else here + tail
                    if k > 0:
                        shifted = tail * float(k * 8)
                        across = shifted if across is None else across + shifted
                out.append((total + here, sum_x + (across + here * (sub + start)), sum_y))
            return tuple(out)

        def settle(tops):
            return tuple(jnp.broadcast_to(jnp.max(t, axis=0, keepdims=True), t.shape) for t in tops)

        def finish(step, peaks, sums):
            f, pair = divmod(step, pairs)
            for m in range(UNITS):
                total, sum_x, sum_y = [jnp.sum(a, axis=0, keepdims=True) for a in sums[m]]
                where_to = lax.rem(pair * UNITS + m + core * half_blocks, blocks)
                out_ref[where_to, f] = jnp.concatenate(
                    [peaks[m][0:1], total, sum_x * (1.0 / W), (sum_y + first_row * total) * (1.0 / total_rows)], axis=0
                )

        stage(0)
        peaks = None
        for step in range(steps + 1):
            f = step // pairs
            new, old = (even, odd) if step % 2 == 0 else (odd, even)

            def part_of(i, state, staged=None):
                tops, sums = state
                if step < steps:
                    if step == 0:
                        pltpu.make_async_copy(
                            feat_ref.at[0, :, pl.ds(0, cols), :], fbuf.at[0, :, pl.ds(0, cols), :], sems.at[0, i]
                        ).wait()
                    feed(f, i, staged)
                if step > 0:
                    sums = weigh(old, i, peaks, sums)
                if step < steps:
                    tops = drain(new, i, tops)
                return tops, sums

            if step == pairs:
                for load in loads[1]:
                    load.wait()
            state = ((low,) * UNITS, ((zero, zero, zero),) * UNITS)
            state = part_of(0, state, 0)
            if step + 1 < steps:
                stage((step + 1) % pairs)
            tops, sums = lax.fori_loop(1, PARTS, part_of, state)
            if step > 0:
                finish(step - 1, peaks, sums)
            if step < steps:
                peaks = settle(tops)

    pl.run_scoped(
        run, *[pltpu.ACC(m)((cols, BLOCK), jnp.float32) for m in range(UNITS) for _ in range(rows_here)]
    )


def score(own, other, features, rows_here):
    frames, pix_count, chan = features.shape
    blocks = 2 * own.shape[0] // BLOCK
    vmem = pl.BlockSpec(memory_space=pltpu.VMEM)
    kept = pltpu.VMEM((PARTS, UNITS, pix_count // PARTS, BLOCK), jnp.float32)
    return pl.pallas_call(
        score_kernel,
        out_shape=jax.ShapeDtypeStruct((blocks, frames, 4, BLOCK), jnp.float32),
        in_specs=[vmem, vmem, pl.BlockSpec(memory_space=pltpu.MemorySpace.HBM)],
        out_specs=vmem,
        scratch_shapes=[
            pltpu.VMEM((frames, rows_here, W, chan), features.dtype),
            kept,
            kept,
            pltpu.SemaphoreType.DMA((frames, PARTS)),
        ],
        compiler_params=pltpu.CompilerParams(vmem_limit_bytes=51 << 20),
        name="score",
    )(own, other, features.reshape(frames, rows_here, W, chan))


def merge_kernel(pixels, parts_ref, inputs_ref, far_ref, near_ref):
    tiles, frames = parts_ref.shape[0], parts_ref.shape[1]
    for f in range(frames):
        parts = [parts_ref[k, f] for k in range(tiles)]
        peak = functools.reduce(jnp.maximum, [p[0:1] for p in parts])
        sums = functools.reduce(jnp.add, [p[1:4] * jnp.exp(p[0:1] - peak) for p in parts])
        total = sums[0:1]
        log_total = jnp.log(total)
        here = jnp.concatenate(
            [sums[1:2] / total, sums[2:3] / total, -log_total, peak + log_total - math.log(pixels)], axis=0
        )
        inputs_ref[f] = here
        if f == 0:
            first = here
        if f == frames - 1:
            last = here
    odd = lax.axis_index("frame") % 2 == 1
    far_ref[...] = jnp.where(odd, last, first)
    near_ref[...] = jnp.where(odd, first, last)


def merge(parts, pixels):
    tiles, frames, stats, share = parts.shape
    vmem = pl.BlockSpec(memory_space=pltpu.VMEM)
    edge = jax.ShapeDtypeStruct((stats, share), jnp.float32)
    return pl.pallas_call(
        functools.partial(merge_kernel, pixels),
        out_shape=(jax.ShapeDtypeStruct((frames, stats, share), jnp.float32), edge, edge),
        in_specs=[vmem],
        out_specs=(vmem, vmem, vmem),
        compiler_params=pltpu.CompilerParams(vmem_limit_bytes=4 << 20),
        name="merge",
    )(parts)


def split(array, count):
    parts = []
    for _ in range(count):
        parts.append(array.astype(jnp.bfloat16))
        array = array - parts[-1].astype(jnp.float32)
    return parts


MEET = ((0, 0), (0, 1), (1, 0), (1, 1), (0, 2), (2, 0))
DEPTH = 128


def prepare_kernel(weight_ref, bias_ref, out_weight_ref, taps_ref, last_ref):
    taps, stats, hidden = weight_ref.shape
    rows = jnp.concatenate([weight_ref[k] for k in range(taps)] + [jnp.broadcast_to(bias_ref[...], (4, hidden))], axis=0)
    thirds = [p.astype(jnp.float32) for p in split(rows, 3)]
    stacked = jnp.concatenate([thirds[i] for i, _ in MEET], axis=0)
    filler = jnp.zeros((DEPTH - stacked.shape[0], hidden), jnp.float32)
    taps_ref[...] = jnp.transpose(jnp.concatenate([stacked, filler], axis=0)).astype(jnp.bfloat16)
    thirds = [p.astype(jnp.float32) for p in split(out_weight_ref[...], 2)]
    filler = jnp.zeros((8 - out_weight_ref.shape[0], hidden), jnp.float32)
    last_ref[...] = jnp.concatenate([thirds[0], filler, thirds[1], filler], axis=0).astype(jnp.bfloat16)


def prepare(conv_weight, conv_bias, out_weight):
    hidden = conv_bias.shape[0]
    vmem = pl.BlockSpec(memory_space=pltpu.VMEM)
    return pl.pallas_call(
        prepare_kernel,
        out_shape=(
            jax.ShapeDtypeStruct((hidden, DEPTH), jnp.bfloat16),
            jax.ShapeDtypeStruct((16, hidden), jnp.bfloat16),
        ),
        in_specs=[vmem] * 3,
        out_specs=(vmem, vmem),
        cost_estimate=pl.CostEstimate(flops=200000, bytes_accessed=200000, transcendentals=0),
        compiler_params=pltpu.CompilerParams(vmem_limit_bytes=8 << 20),
        name="prepare",
    )(conv_weight, conv_bias[None, :], out_weight)


def refine_kernel(far_ref, inputs_ref, near_ref, taps_ref, last_ref, out_ref, held, sem):
    frames, share = inputs_ref.shape[0], inputs_ref.shape[2]
    odd = lax.axis_index("frame") % 2 == 1
    far, near = far_ref[...], near_ref[...]
    before, after = jnp.where(odd, near, far), jnp.where(odd, far, near)
    line = [before] + [inputs_ref[f] for f in range(frames)] + [after]
    unit = jnp.where(lax.broadcasted_iota(jnp.int32, (4, share), 0) == 0, 1.0, 0.0)
    right = []
    for f in range(frames):
        rows = jnp.concatenate([line[f + k] for k in range(3)] + [unit], axis=0)
        thirds = [p.astype(jnp.float32) for p in split(rows, 3)]
        stacked = jnp.concatenate([thirds[j] for _, j in MEET], axis=0)
        filler = jnp.zeros((DEPTH - stacked.shape[0], share), jnp.float32)
        right.append(jnp.concatenate([stacked, filler], axis=0).astype(jnp.bfloat16))
    for f in range(frames):
        acc = jnp.dot(taps_ref[...], right[f], preferred_element_type=jnp.float32)
        hidden = jax.nn.gelu(acc)
        high, rest = split(hidden, 2)
        first = jnp.dot(last_ref[...], high, preferred_element_type=jnp.float32)
        second = jnp.dot(last_ref[...], rest, preferred_element_type=jnp.float32)
        delta = first[0:3] + (first[8:11] + second[0:3])
        moved = line[f + 1][0:3] + delta
        for o in range(3):
            held[o, f : f + 1] = moved[o : o + 1]
    store = pltpu.make_async_copy(held, out_ref, sem)
    store.start()
    store.wait()


def refine(far, inputs, near, taps, last):
    frames, _, share = inputs.shape
    moved = pl.pallas_call(
        refine_kernel,
        out_shape=jax.ShapeDtypeStruct((3, frames, share), jnp.float32),
        in_specs=[pl.BlockSpec(memory_space=pltpu.VMEM)] * 5,
        out_specs=pl.BlockSpec(memory_space=pltpu.MemorySpace.HBM),
        scratch_shapes=[pltpu.VMEM((3, frames, share), jnp.float32), pltpu.SemaphoreType.DMA],
        compiler_params=pltpu.CompilerParams(vmem_limit_bytes=8 << 20),
        name="refine",
    )(far, inputs, near, taps, last)
    return jnp.transpose(moved, (1, 0, 2))


def local(features, query_frame, query_row, query_col, conv_weight, conv_bias, out_weight):
    frame_count, pix_count, chan = features.shape
    rows_here = pix_count // W
    tiles, groups = lax.axis_size("tile"), lax.axis_size("frame")
    plane, column = mesh_groups()
    keep, send = pick(features, query_frame, query_row, query_col, rows_here)
    swap = [(i, i ^ 1) for i in range(tiles)]
    mine = keep + lax.ppermute(send, "tile", swap)
    wide, tall = len(plane[0]), len(column[0])
    rows = mine.shape[0] // wide
    got = lax.all_to_all(mine.reshape(wide, rows, chan), "frame", 0, 0, axis_index_groups=plane)
    piece = jnp.sum(got, axis=0)
    got = lax.all_to_all(jnp.broadcast_to(piece, (tall, rows, chan)), BOTH, 0, 0, axis_index_groups=column)
    piece = jnp.sum(got, axis=0)
    got = lax.all_to_all(jnp.broadcast_to(piece, (wide, rows, chan)), "frame", 0, 0, axis_index_groups=plane)
    own = got.reshape(wide * rows, chan)
    other = lax.ppermute(own, "tile", swap)
    parts = score(own, other, features, rows_here)
    parts = lax.all_to_all(parts, "tile", 0, 0)
    inputs, far, near = merge(parts, rows_here * tiles * W)
    far = lax.ppermute(far, "frame", [p for i in range(1, groups - 1, 2) for p in ((i, i + 1), (i + 1, i))])
    near = lax.ppermute(near, "frame", [(i, i ^ 1) for i in range(groups)])
    taps, last_weight = prepare(conv_weight, conv_bias, out_weight)
    return refine(far, inputs, near, taps, last_weight)


def solution(mesh):
    in_specs = (P("frame", "tile", None), P(), P(), P(), P(), P(), P())
    out_specs = P("frame", None, "tile")
    return jax.shard_map(local, mesh=mesh, in_specs=in_specs, out_specs=out_specs, check_vma=False)
```

```python
import functools
import math

import jax
import jax.numpy as jnp
from jax import lax
from jax.experimental import pallas as pl
from jax.experimental.pallas import tpu as pltpu
from jax.sharding import PartitionSpec as P

W = 480
LOG2E = math.log2(math.e)
BOTH = ("frame", "tile")


def mesh_groups():
    plane = [[x * 8 + zh * 4 + y for x in range(4) for y in range(4)] for zh in range(2)]
    column = [
        [(x * 8 + zh * 4 + y) * 8 + zl * 2 + c for zh in range(2) for zl in range(4)]
        for x in range(4)
        for y in range(4)
        for c in range(2)
    ]
    return plane, column


BATCH = 4


def pick_kernel(rows_here, idx_ref, feat_ref, keep_ref, send_ref, vm, sm, found_at, slots, wide, lines, sems, sem):
    frame_idx, tile_idx = lax.axis_index("frame"), lax.axis_index("tile")
    core = tile_idx % 2
    pix_count = rows_here * W
    frame_count = feat_ref.shape[0] // pix_count
    half = keep_ref.shape[0]
    sets, groups = idx_ref.shape
    lines[...] = jnp.zeros_like(lines)
    frame = jnp.right_shift(idx_ref[...], 18) - frame_idx * frame_count
    row = (jnp.right_shift(idx_ref[...], 9) & 511) - tile_idx * rows_here
    owned = (frame >= 0) & (frame < frame_count) & (row >= 0) & (row < rows_here)
    vm[0:sets, :] = frame * pix_count + row * W + (idx_ref[...] & 511)
    bit = lax.broadcasted_iota(jnp.int32, owned.shape, 0)
    word = jnp.sum(jnp.where(owned, jnp.left_shift(1, bit), 0), axis=0, keepdims=True)
    word = word | jnp.left_shift(pltpu.roll(word, groups // 2, axis=1), sets)
    vm[sets : sets + 8, :] = jnp.broadcast_to(word, (8, groups))
    to_scalar = pltpu.make_async_copy(vm, sm, sems)
    to_scalar.start()
    to_scalar.wait()

    def copy(k, pix):
        first = pl.multiple_of(pix & ~15, 16)
        return pltpu.make_async_copy(
            feat_ref.at[pl.ds(first, 16), :], slots.at[pl.ds(pl.multiple_of(k * 16, 16), 16), :], sem
        )

    def group(g, count):
        def step(state):
            left, count = state
            i = 31 - lax.clz(left & -left)
            at, lane = i & (sets - 1), g + lax.shift_right_logical(i, sets.bit_length() - 1) * (groups // 2)
            pix = sm[at, lane]
            copy(count, pix).start()
            found_at[0, count] = at * groups + lane
            found_at[1, count] = pix & 15
            return left & (left - 1), count + 1

        return lax.while_loop(lambda state: state[0] != 0, step, (sm[sets, g], count))[1]

    found = lax.fori_loop(0, groups // 2, group, 0)
    for k in range(BATCH - 1):
        found_at[0, found + k] = lines.shape[0] - 8
        found_at[1, found + k] = 0

    def wait(rows):
        def step(k, carry):
            pltpu.make_async_copy(feat_ref.at[pl.ds(0, rows), :], slots.at[pl.ds(0, rows), :], sem).wait()
            return carry

        return step

    lax.fori_loop(0, lax.shift_right_logical(found, 3), wait(128), 0)
    lax.fori_loop(0, found & 7, wait(16), 0)

    def place(batch, carry):
        for k in range(BATCH):
            at = pl.multiple_of((batch * BATCH + k) * 16, 16)
            wide[k] = slots[pl.ds(at, 16), :].astype(jnp.float32)
        picked = [wide[k, pl.ds(found_at[1, batch * BATCH + k], 1), :] for k in range(BATCH)]
        for k in range(BATCH):
            lines[pl.ds(found_at[0, batch * BATCH + k], 1), :] = picked[k]
        return carry

    lax.fori_loop(0, lax.div(found + BATCH - 1, BATCH), place, 0)
    mine = pl.multiple_of(core * half, half)
    theirs = pl.multiple_of((1 - core) * half, half)
    keep_ref[...] = (lines[pl.ds(mine, half), :] * 0.0625).astype(keep_ref.dtype)
    send_ref[...] = (lines[pl.ds(theirs, half), :] * 0.0625).astype(send_ref.dtype)


def pick(features, query_frame, query_row, query_col, rows_here):
    flat = features.reshape(-1, features.shape[2])
    queries, chan = query_frame.shape[0], features.shape[2]
    lanes = 128
    sets = queries // lanes
    half = jax.ShapeDtypeStruct((queries // 2, chan), features.dtype)
    vmem = pl.BlockSpec(memory_space=pltpu.VMEM)
    hbm = pl.BlockSpec(memory_space=pltpu.MemorySpace.HBM)
    return pl.pallas_call(
        functools.partial(pick_kernel, rows_here),
        out_shape=(half, half),
        in_specs=[vmem, hbm],
        out_specs=(vmem, vmem),
        scratch_shapes=[
            pltpu.VMEM((sets + 8, lanes), jnp.int32),
            pltpu.SMEM((sets + 8, lanes), jnp.int32),
            pltpu.SMEM((2, queries + BATCH), jnp.int32),
            pltpu.VMEM(((queries + BATCH) * 16, chan), features.dtype),
            pltpu.VMEM((BATCH, 16, chan), jnp.float32),
            pltpu.VMEM((queries + 8, chan), jnp.float32),
            pltpu.SemaphoreType.DMA,
            pltpu.SemaphoreType.DMA,
        ],
        compiler_params=pltpu.CompilerParams(vmem_limit_bytes=51 << 20),
        name="pick",
    )((query_frame * 2**18 + query_row * 2**9 + query_col).reshape(sets, lanes), flat)


BLOCK = 256
PARTS = 5
UNITS = 2


def score_kernel(own_ref, other_ref, feat_ref, out_ref, fbuf, even, odd, sems):
    tile_idx = lax.axis_index("tile")
    core = tile_idx % 2
    frames, rows_here = fbuf.shape[0], fbuf.shape[1]
    cols = W // PARTS
    loads = [
        [
            pltpu.make_async_copy(
                feat_ref.at[f, :, pl.ds(i * cols, cols), :], fbuf.at[f, :, pl.ds(i * cols, cols), :], sems.at[f, i]
            )
            for i in range(PARTS)
        ]
        for f in range(frames)
    ]
    for load in loads[0] + loads[1]:
        load.start()
    half_blocks = own_ref.shape[0] // BLOCK
    blocks = 2 * half_blocks
    pairs = blocks // UNITS
    steps = frames * pairs
    total_rows = float(rows_here * lax.axis_size("tile"))
    first_row = (tile_idx * rows_here).astype(jnp.float32)
    sub = lax.broadcasted_iota(jnp.int32, (8, BLOCK), 0).astype(jnp.float32)
    zero = jnp.zeros((8, BLOCK), jnp.float32)
    low = jnp.full((8, BLOCK), -jnp.inf, jnp.float32)

    def stage(pair):
        for m in range(UNITS):
            ref, k = (own_ref, pair * UNITS + m) if pair * UNITS < half_blocks else (other_ref, pair * UNITS + m - half_blocks)
            pltpu.matmul_push_rhs(ref[k * BLOCK : (k + 1) * BLOCK, :], 0, m, transpose=True)

    def run(*accs):
        def moves(f, part, staged, kept, was, tops):
            for r in range(rows_here):
                seen = None if tops is None else []
                if tops is not None:
                    for m in range(UNITS):
                        scores = pltpu.matmul_pop(accs[m * rows_here + r])
                        kept[was, m, r * cols : (r + 1) * cols, :] = scores
                        tops[m] = jnp.maximum(tops[m], jnp.max(scores.reshape(cols // 8, 8, BLOCK), axis=0))
                        seen.append(scores[cols - 8 : cols, :])
                if f is not None:
                    lhs = fbuf[f, r, pl.ds(pl.multiple_of(part * cols, 16), cols), :]
                    for m in range(UNITS):
                        pltpu.matmul_acc_lhs(accs[m * rows_here + r], lhs, load_staged_rhs=staged if r == 0 else None)
                yield seen

        def weighs(kept, part, peaks, sums):
            start = jnp.asarray(part * cols).astype(jnp.float32)
            here, across = [None] * UNITS, [None] * UNITS
            for k in range(cols // 8):
                for m in range(UNITS):
                    tail, below = None, None
                    for r in reversed(range(rows_here)):
                        at = r * cols + k * 8
                        expo = jnp.exp2((kept[part, m, at : at + 8, :] - peaks[m]) * LOG2E)
                        tail = expo if tail is None else tail + expo
                        if r > 0:
                            below = tail if below is None else below + tail
                    sums[m][2] = sums[m][2] + below
                    here[m] = tail if here[m] is None else here[m] + tail
                    if k > 0:
                        shifted = tail * float(k * 8)
                        across[m] = shifted if across[m] is None else across[m] + shifted
                    yield
            for m in range(UNITS):
                sums[m][0] = sums[m][0] + here[m]
                sums[m][1] = sums[m][1] + (across[m] + here[m] * (sub + start))

        def weave(moving, weighing, peaks):
            per = (cols // 8) * UNITS // rows_here
            if moving is None:
                moving = iter(())
            if weighing is None:
                weighing = iter(())
            for _ in range(rows_here):
                seen = next(moving, None)
                if seen is not None and peaks is not None:
                    for m in range(UNITS):
                        peaks[m] = jnp.minimum(peaks[m], jnp.maximum(peaks[m], seen[m]))
                for _ in range(per):
                    next(weighing, None)
            for _ in moving:
                pass
            for _ in weighing:
                pass

        def settle(tops):
            return tuple(jnp.broadcast_to(jnp.max(t, axis=0, keepdims=True), t.shape) for t in tops)

        def finish(step, peaks, sums):
            f, pair = divmod(step, pairs)
            for m in range(UNITS):
                total, sum_x, sum_y = [jnp.sum(a, axis=0, keepdims=True) for a in sums[m]]
                where_to = lax.rem(pair * UNITS + m + core * half_blocks, blocks)
                out_ref[where_to, f] = jnp.concatenate(
                    [peaks[m][0:1], total, sum_x * (1.0 / W), (sum_y + first_row * total) * (1.0 / total_rows)], axis=0
                )

        none, fresh = (low,) * UNITS, ((zero, zero, zero),) * UNITS
        stage(0)
        loads[0][0].wait()
        tops, peaks, sums = None, None, None
        for step in range(steps + 2):
            f = step // pairs if step < steps else None
            new, old = (even, odd) if step % 2 == 0 else (odd, even)
            if step == pairs:
                for load in loads[1]:
                    load.wait()
            last_peaks = peaks
            tops = None if tops is None else list(tops)
            sums = None if sums is None else [list(x) for x in sums]
            bound = None if last_peaks is None else list(last_peaks)
            weave(
                moves(f, 0, 0, old, PARTS - 1, tops) if step <= steps else None,
                weighs(new, PARTS - 1, bound, sums) if step > 1 else None,
                bound,
            )
            if step <= steps:
                peaks = None if tops is None else settle(tops)
            if step + 1 < steps:
                stage((step + 1) % pairs)
            if step > 1:
                finish(step - 2, last_peaks, sums)
            if step > steps:
                break

            def part_of(i, state):
                tops, sums = state
                if step == 0:
                    pltpu.make_async_copy(
                        feat_ref.at[0, :, pl.ds(0, cols), :], fbuf.at[0, :, pl.ds(0, cols), :], sems.at[0, i]
                    ).wait()
                tops, sums = list(tops), [list(x) for x in sums]
                bound = None if peaks is None else list(peaks)
                weave(
                    moves(f, i, None, new, i - 1, tops) if step < steps else None,
                    weighs(old, i - 1, bound, sums) if step > 0 else None,
                    bound,
                )
                tops, sums = tuple(tops), tuple(tuple(x) for x in sums)
                return tops, sums

            tops, sums = lax.fori_loop(1, PARTS, part_of, (none, fresh))

    pl.run_scoped(
        run, *[pltpu.ACC(m)((cols, BLOCK), jnp.float32) for m in range(UNITS) for _ in range(rows_here)]
    )


def score(own, other, features, rows_here):
    frames, pix_count, chan = features.shape
    blocks = 2 * own.shape[0] // BLOCK
    vmem = pl.BlockSpec(memory_space=pltpu.VMEM)
    kept = pltpu.VMEM((PARTS, UNITS, pix_count // PARTS, BLOCK), jnp.float32)
    return pl.pallas_call(
        score_kernel,
        out_shape=jax.ShapeDtypeStruct((blocks, frames, 4, BLOCK), jnp.float32),
        in_specs=[vmem, vmem, pl.BlockSpec(memory_space=pltpu.MemorySpace.HBM)],
        out_specs=vmem,
        scratch_shapes=[
            pltpu.VMEM((frames, rows_here, W, chan), features.dtype),
            kept,
            kept,
            pltpu.SemaphoreType.DMA((frames, PARTS)),
        ],
        compiler_params=pltpu.CompilerParams(vmem_limit_bytes=51 << 20),
        name="score",
    )(own, other, features.reshape(frames, rows_here, W, chan))


def merge_kernel(pixels, parts_ref, inputs_ref, far_ref, near_ref):
    tiles, frames = parts_ref.shape[0], parts_ref.shape[1]
    for f in range(frames):
        parts = [parts_ref[k, f] for k in range(tiles)]
        peak = functools.reduce(jnp.maximum, [p[0:1] for p in parts])
        sums = functools.reduce(jnp.add, [p[1:4] * jnp.exp(p[0:1] - peak) for p in parts])
        total = sums[0:1]
        log_total = jnp.log(total)
        here = jnp.concatenate(
            [sums[1:2] / total, sums[2:3] / total, -log_total, peak + log_total - math.log(pixels)], axis=0
        )
        inputs_ref[f] = here
        if f == 0:
            first = here
        if f == frames - 1:
            last = here
    odd = lax.axis_index("frame") % 2 == 1
    far_ref[...] = jnp.where(odd, last, first)
    near_ref[...] = jnp.where(odd, first, last)


def merge(parts, pixels):
    tiles, frames, stats, share = parts.shape
    vmem = pl.BlockSpec(memory_space=pltpu.VMEM)
    edge = jax.ShapeDtypeStruct((stats, share), jnp.float32)
    return pl.pallas_call(
        functools.partial(merge_kernel, pixels),
        out_shape=(jax.ShapeDtypeStruct((frames, stats, share), jnp.float32), edge, edge),
        in_specs=[vmem],
        out_specs=(vmem, vmem, vmem),
        compiler_params=pltpu.CompilerParams(vmem_limit_bytes=4 << 20),
        name="merge",
    )(parts)


def split(array, count):
    parts = []
    for _ in range(count):
        parts.append(array.astype(jnp.bfloat16))
        array = array - parts[-1].astype(jnp.float32)
    return parts


MEET = ((0, 0), (0, 1), (1, 0), (1, 1), (0, 2), (2, 0))
DEPTH = 128


def prepare_kernel(weight_ref, bias_ref, out_weight_ref, taps_ref, last_ref):
    taps, stats, hidden = weight_ref.shape
    rows = jnp.concatenate([weight_ref[k] for k in range(taps)] + [jnp.broadcast_to(bias_ref[...], (4, hidden))], axis=0)
    thirds = [p.astype(jnp.float32) for p in split(rows, 3)]
    stacked = jnp.concatenate([thirds[i] for i, _ in MEET], axis=0)
    filler = jnp.zeros((DEPTH - stacked.shape[0], hidden), jnp.float32)
    taps_ref[...] = jnp.transpose(jnp.concatenate([stacked, filler], axis=0)).astype(jnp.bfloat16)
    thirds = [p.astype(jnp.float32) for p in split(out_weight_ref[...], 2)]
    filler = jnp.zeros((8 - out_weight_ref.shape[0], hidden), jnp.float32)
    last_ref[...] = jnp.concatenate([thirds[0], filler, thirds[1], filler], axis=0).astype(jnp.bfloat16)


def prepare(conv_weight, conv_bias, out_weight):
    hidden = conv_bias.shape[0]
    vmem = pl.BlockSpec(memory_space=pltpu.VMEM)
    return pl.pallas_call(
        prepare_kernel,
        out_shape=(
            jax.ShapeDtypeStruct((hidden, DEPTH), jnp.bfloat16),
            jax.ShapeDtypeStruct((16, hidden), jnp.bfloat16),
        ),
        in_specs=[vmem] * 3,
        out_specs=(vmem, vmem),
        cost_estimate=pl.CostEstimate(flops=200000, bytes_accessed=200000, transcendentals=0),
        compiler_params=pltpu.CompilerParams(vmem_limit_bytes=8 << 20),
        name="prepare",
    )(conv_weight, conv_bias[None, :], out_weight)


def refine_kernel(far_ref, inputs_ref, near_ref, taps_ref, last_ref, out_ref, held, sem):
    frames, share = inputs_ref.shape[0], inputs_ref.shape[2]
    odd = lax.axis_index("frame") % 2 == 1
    far, near = far_ref[...], near_ref[...]
    before, after = jnp.where(odd, near, far), jnp.where(odd, far, near)
    line = [before] + [inputs_ref[f] for f in range(frames)] + [after]
    unit = jnp.where(lax.broadcasted_iota(jnp.int32, (4, share), 0) == 0, 1.0, 0.0)
    right = []
    for f in range(frames):
        rows = jnp.concatenate([line[f + k] for k in range(3)] + [unit], axis=0)
        thirds = [p.astype(jnp.float32) for p in split(rows, 3)]
        stacked = jnp.concatenate([thirds[j] for _, j in MEET], axis=0)
        filler = jnp.zeros((DEPTH - stacked.shape[0], share), jnp.float32)
        right.append(jnp.concatenate([stacked, filler], axis=0).astype(jnp.bfloat16))
    for f in range(frames):
        acc = jnp.dot(taps_ref[...], right[f], preferred_element_type=jnp.float32)
        hidden = jax.nn.gelu(acc)
        high, rest = split(hidden, 2)
        first = jnp.dot(last_ref[...], high, preferred_element_type=jnp.float32)
        second = jnp.dot(last_ref[...], rest, preferred_element_type=jnp.float32)
        delta = first[0:3] + (first[8:11] + second[0:3])
        moved = line[f + 1][0:3] + delta
        for o in range(3):
            held[o, f : f + 1] = moved[o : o + 1]
    store = pltpu.make_async_copy(held, out_ref, sem)
    store.start()
    store.wait()


def refine(far, inputs, near, taps, last):
    frames, _, share = inputs.shape
    moved = pl.pallas_call(
        refine_kernel,
        out_shape=jax.ShapeDtypeStruct((3, frames, share), jnp.float32),
        in_specs=[pl.BlockSpec(memory_space=pltpu.VMEM)] * 5,
        out_specs=pl.BlockSpec(memory_space=pltpu.MemorySpace.HBM),
        scratch_shapes=[pltpu.VMEM((3, frames, share), jnp.float32), pltpu.SemaphoreType.DMA],
        compiler_params=pltpu.CompilerParams(vmem_limit_bytes=8 << 20),
        name="refine",
    )(far, inputs, near, taps, last)
    return jnp.transpose(moved, (1, 0, 2))


def local(features, query_frame, query_row, query_col, conv_weight, conv_bias, out_weight):
    frame_count, pix_count, chan = features.shape
    rows_here = pix_count // W
    tiles, groups = lax.axis_size("tile"), lax.axis_size("frame")
    plane, column = mesh_groups()
    keep, send = pick(features, query_frame, query_row, query_col, rows_here)
    swap = [(i, i ^ 1) for i in range(tiles)]
    mine = keep + lax.ppermute(send, "tile", swap)
    wide, tall = len(plane[0]), len(column[0])
    rows = mine.shape[0] // wide
    got = lax.all_to_all(mine.reshape(wide, rows, chan), "frame", 0, 0, axis_index_groups=plane)
    piece = jnp.sum(got, axis=0)
    got = lax.all_to_all(jnp.broadcast_to(piece, (tall, rows, chan)), BOTH, 0, 0, axis_index_groups=column)
    piece = jnp.sum(got, axis=0)
    got = lax.all_to_all(jnp.broadcast_to(piece, (wide, rows, chan)), "frame", 0, 0, axis_index_groups=plane)
    own = got.reshape(wide * rows, chan)
    other = lax.ppermute(own, "tile", swap)
    parts = score(own, other, features, rows_here)
    parts = lax.all_to_all(parts, "tile", 0, 0)
    inputs, far, near = merge(parts, rows_here * tiles * W)
    far = lax.ppermute(far, "frame", [p for i in range(1, groups - 1, 2) for p in ((i, i + 1), (i + 1, i))])
    near = lax.ppermute(near, "frame", [(i, i ^ 1) for i in range(groups)])
    taps, last_weight = prepare(conv_weight, conv_bias, out_weight)
    return refine(far, inputs, near, taps, last_weight)


def solution(mesh):
    in_specs = (P("frame", "tile", None), P(), P(), P(), P(), P(), P())
    out_specs = P("frame", None, "tile")
    return jax.shard_map(local, mesh=mesh, in_specs=in_specs, out_specs=out_specs, check_vma=False)
```

```python
import functools
import math

import jax
import jax.numpy as jnp
from jax import lax
from jax.experimental import pallas as pl
from jax.experimental.pallas import tpu as pltpu
from jax.sharding import PartitionSpec as P

W = 480
LOG2E = math.log2(math.e)
BOTH = ("frame", "tile")


def mesh_groups():
    plane = [[x * 8 + zh * 4 + y for x in range(4) for y in range(4)] for zh in range(2)]
    column = [
        [(x * 8 + zh * 4 + y) * 8 + zl * 2 + c for zh in range(2) for zl in range(4)]
        for x in range(4)
        for y in range(4)
        for c in range(2)
    ]
    couple = [[(f % 32) * 8 + t for f in (i, i + 1) for t in range(8)] for i in range(1, 32, 2)]
    return plane, column, couple


BATCH = 4


def pick_kernel(rows_here, idx_ref, feat_ref, keep_ref, send_ref, vm, sm, found_at, slots, wide, lines, sems, sem):
    frame_idx, tile_idx = lax.axis_index("frame"), lax.axis_index("tile")
    core = tile_idx % 2
    pix_count = rows_here * W
    frame_count = feat_ref.shape[0] // pix_count
    half = keep_ref.shape[0]
    sets, groups = idx_ref.shape
    lines[...] = jnp.zeros_like(lines)
    frame = jnp.right_shift(idx_ref[...], 18) - frame_idx * frame_count
    row = (jnp.right_shift(idx_ref[...], 9) & 511) - tile_idx * rows_here
    owned = (frame >= 0) & (frame < frame_count) & (row >= 0) & (row < rows_here)
    vm[0:sets, :] = frame * pix_count + row * W + (idx_ref[...] & 511)
    bit = lax.broadcasted_iota(jnp.int32, owned.shape, 0)
    word = jnp.sum(jnp.where(owned, jnp.left_shift(1, bit), 0), axis=0, keepdims=True)
    word = word | jnp.left_shift(pltpu.roll(word, groups // 2, axis=1), sets)
    vm[sets : sets + 8, :] = jnp.broadcast_to(word, (8, groups))
    to_scalar = pltpu.make_async_copy(vm, sm, sems)
    to_scalar.start()
    to_scalar.wait()

    def copy(k, pix):
        first = pl.multiple_of(pix & ~15, 16)
        return pltpu.make_async_copy(
            feat_ref.at[pl.ds(first, 16), :], slots.at[pl.ds(pl.multiple_of(k * 16, 16), 16), :], sem
        )

    def group(g, count):
        def step(state):
            left, count = state
            i = 31 - lax.clz(left & -left)
            at, lane = i & (sets - 1), g + lax.shift_right_logical(i, sets.bit_length() - 1) * (groups // 2)
            pix = sm[at, lane]
            copy(count, pix).start()
            found_at[0, count] = at * groups + lane
            found_at[1, count] = pix & 15
            return left & (left - 1), count + 1

        return lax.while_loop(lambda state: state[0] != 0, step, (sm[sets, g], count))[1]

    found = lax.fori_loop(0, groups // 2, group, 0)
    for k in range(BATCH - 1):
        found_at[0, found + k] = lines.shape[0] - 8
        found_at[1, found + k] = 0

    def wait(rows):
        def step(k, carry):
            pltpu.make_async_copy(feat_ref.at[pl.ds(0, rows), :], slots.at[pl.ds(0, rows), :], sem).wait()
            return carry

        return step

    lax.fori_loop(0, lax.shift_right_logical(found, 3), wait(128), 0)
    lax.fori_loop(0, found & 7, wait(16), 0)

    def place(batch, carry):
        for k in range(BATCH):
            at = pl.multiple_of((batch * BATCH + k) * 16, 16)
            wide[k] = slots[pl.ds(at, 16), :].astype(jnp.float32)
        picked = [wide[k, pl.ds(found_at[1, batch * BATCH + k], 1), :] for k in range(BATCH)]
        for k in range(BATCH):
            lines[pl.ds(found_at[0, batch * BATCH + k], 1), :] = picked[k]
        return carry

    lax.fori_loop(0, lax.div(found + BATCH - 1, BATCH), place, 0)
    mine = pl.multiple_of(core * half, half)
    theirs = pl.multiple_of((1 - core) * half, half)
    keep_ref[...] = (lines[pl.ds(mine, half), :] * 0.0625).astype(keep_ref.dtype)
    send_ref[...] = (lines[pl.ds(theirs, half), :] * 0.0625).astype(send_ref.dtype)


def pick(features, query_frame, query_row, query_col, rows_here):
    flat = features.reshape(-1, features.shape[2])
    queries, chan = query_frame.shape[0], features.shape[2]
    lanes = 128
    sets = queries // lanes
    half = jax.ShapeDtypeStruct((queries // 2, chan), features.dtype)
    vmem = pl.BlockSpec(memory_space=pltpu.VMEM)
    hbm = pl.BlockSpec(memory_space=pltpu.MemorySpace.HBM)
    return pl.pallas_call(
        functools.partial(pick_kernel, rows_here),
        out_shape=(half, half),
        in_specs=[vmem, hbm],
        out_specs=(vmem, vmem),
        scratch_shapes=[
            pltpu.VMEM((sets + 8, lanes), jnp.int32),
            pltpu.SMEM((sets + 8, lanes), jnp.int32),
            pltpu.SMEM((2, queries + BATCH), jnp.int32),
            pltpu.VMEM(((queries + BATCH) * 16, chan), features.dtype),
            pltpu.VMEM((BATCH, 16, chan), jnp.float32),
            pltpu.VMEM((queries + 8, chan), jnp.float32),
            pltpu.SemaphoreType.DMA,
            pltpu.SemaphoreType.DMA,
        ],
        compiler_params=pltpu.CompilerParams(vmem_limit_bytes=51 << 20),
        name="pick",
    )((query_frame * 2**18 + query_row * 2**9 + query_col).reshape(sets, lanes), flat)


BLOCK = 256
PARTS = 5
UNITS = 2


def score_kernel(own_ref, other_ref, feat_ref, out_ref, fbuf, even, odd, sems):
    tile_idx = lax.axis_index("tile")
    core = tile_idx % 2
    frames, rows_here = fbuf.shape[0], fbuf.shape[1]
    cols = W // PARTS
    loads = [
        [
            pltpu.make_async_copy(
                feat_ref.at[f, :, pl.ds(i * cols, cols), :], fbuf.at[f, :, pl.ds(i * cols, cols), :], sems.at[f, i]
            )
            for i in range(PARTS)
        ]
        for f in range(frames)
    ]
    for load in loads[0] + loads[1]:
        load.start()
    half_blocks = own_ref.shape[0] // BLOCK
    blocks = 2 * half_blocks
    pairs = blocks // UNITS
    steps = frames * pairs
    total_rows = float(rows_here * lax.axis_size("tile"))
    first_row = (tile_idx * rows_here).astype(jnp.float32)
    sub = lax.broadcasted_iota(jnp.int32, (8, BLOCK), 0).astype(jnp.float32)
    zero = jnp.zeros((8, BLOCK), jnp.float32)
    low = jnp.full((8, BLOCK), -jnp.inf, jnp.float32)

    def stage(pair):
        for m in range(UNITS):
            ref, k = (own_ref, pair * UNITS + m) if pair * UNITS < half_blocks else (other_ref, pair * UNITS + m - half_blocks)
            pltpu.matmul_push_rhs(ref[k * BLOCK : (k + 1) * BLOCK, :], 0, m, transpose=True)

    def run(*accs):
        def moves(f, part, staged, kept, was, tops):
            for r in range(rows_here):
                seen = None if tops is None else []
                if tops is not None:
                    for m in range(UNITS):
                        scores = pltpu.matmul_pop(accs[m * rows_here + r])
                        kept[was, m, r * cols : (r + 1) * cols, :] = scores
                        tops[m] = jnp.maximum(tops[m], jnp.max(scores.reshape(cols // 8, 8, BLOCK), axis=0))
                        seen.append(scores[cols - 8 : cols, :])
                if f is not None:
                    lhs = fbuf[f, r, pl.ds(pl.multiple_of(part * cols, 16), cols), :]
                    for m in range(UNITS):
                        pltpu.matmul_acc_lhs(accs[m * rows_here + r], lhs, load_staged_rhs=staged if r == 0 else None)
                yield seen

        def weighs(kept, part, peaks, sums):
            start = jnp.asarray(part * cols).astype(jnp.float32)
            here, across = [None] * UNITS, [None] * UNITS
            for k in range(cols // 8):
                for m in range(UNITS):
                    tail, below = None, None
                    for r in reversed(range(rows_here)):
                        at = r * cols + k * 8
                        expo = jnp.exp2((kept[part, m, at : at + 8, :] - peaks[m]) * LOG2E)
                        tail = expo if tail is None else tail + expo
                        if r > 0:
                            below = tail if below is None else below + tail
                    sums[m][2] = sums[m][2] + below
                    here[m] = tail if here[m] is None else here[m] + tail
                    if k > 0:
                        shifted = tail * float(k * 8)
                        across[m] = shifted if across[m] is None else across[m] + shifted
                    yield
            for m in range(UNITS):
                sums[m][0] = sums[m][0] + here[m]
                sums[m][1] = sums[m][1] + (across[m] + here[m] * (sub + start))

        def weave(moving, weighing, peaks):
            per = (cols // 8) * UNITS // rows_here
            if moving is None:
                moving = iter(())
            if weighing is None:
                weighing = iter(())
            for _ in range(rows_here):
                seen = next(moving, None)
                if seen is not None and peaks is not None:
                    for m in range(UNITS):
                        peaks[m] = jnp.minimum(peaks[m], jnp.maximum(peaks[m], seen[m]))
                for _ in range(per):
                    next(weighing, None)
            for _ in moving:
                pass
            for _ in weighing:
                pass

        def settle(tops):
            return tuple(jnp.broadcast_to(jnp.max(t, axis=0, keepdims=True), t.shape) for t in tops)

        def finish(step, peaks, sums):
            f, pair = divmod(step, pairs)
            for m in range(UNITS):
                total, sum_x, sum_y = [jnp.sum(a, axis=0, keepdims=True) for a in sums[m]]
                where_to = lax.rem(pair * UNITS + m + core * half_blocks, blocks)
                packed = jnp.concatenate(
                    [peaks[m][0:1], total, sum_x * (1.0 / W), (sum_y + first_row * total) * (1.0 / total_rows)], axis=0
                )
                for side in range(2):
                    out_ref[side, where_to, f] = packed

        none, fresh = (low,) * UNITS, ((zero, zero, zero),) * UNITS
        stage(0)
        loads[0][0].wait()
        tops, peaks, sums = None, None, None
        for step in range(steps + 2):
            f = step // pairs if step < steps else None
            new, old = (even, odd) if step % 2 == 0 else (odd, even)
            if step == pairs:
                for load in loads[1]:
                    load.wait()
            last_peaks = peaks
            tops = None if tops is None else list(tops)
            sums = None if sums is None else [list(x) for x in sums]
            bound = None if last_peaks is None else list(last_peaks)
            weave(
                moves(f, 0, 0, old, PARTS - 1, tops) if step <= steps else None,
                weighs(new, PARTS - 1, bound, sums) if step > 1 else None,
                bound,
            )
            if step <= steps:
                peaks = None if tops is None else settle(tops)
            if step + 1 < steps:
                stage((step + 1) % pairs)
            if step > 1:
                finish(step - 2, last_peaks, sums)
            if step > steps:
                break

            def part_of(i, state):
                tops, sums = state
                if step == 0:
                    pltpu.make_async_copy(
                        feat_ref.at[0, :, pl.ds(0, cols), :], fbuf.at[0, :, pl.ds(0, cols), :], sems.at[0, i]
                    ).wait()
                tops, sums = list(tops), [list(x) for x in sums]
                bound = None if peaks is None else list(peaks)
                weave(
                    moves(f, i, None, new, i - 1, tops) if step < steps else None,
                    weighs(old, i - 1, bound, sums) if step > 0 else None,
                    bound,
                )
                tops, sums = tuple(tops), tuple(tuple(x) for x in sums)
                return tops, sums

            tops, sums = lax.fori_loop(1, PARTS, part_of, (none, fresh))

    pl.run_scoped(
        run, *[pltpu.ACC(m)((cols, BLOCK), jnp.float32) for m in range(UNITS) for _ in range(rows_here)]
    )


def score(own, other, features, rows_here):
    frames, pix_count, chan = features.shape
    blocks = 2 * own.shape[0] // BLOCK
    vmem = pl.BlockSpec(memory_space=pltpu.VMEM)
    kept = pltpu.VMEM((PARTS, UNITS, pix_count // PARTS, BLOCK), jnp.float32)
    return pl.pallas_call(
        score_kernel,
        out_shape=jax.ShapeDtypeStruct((2, blocks, frames, 4, BLOCK), jnp.float32),
        in_specs=[vmem, vmem, pl.BlockSpec(memory_space=pltpu.MemorySpace.HBM)],
        out_specs=vmem,
        scratch_shapes=[
            pltpu.VMEM((frames, rows_here, W, chan), features.dtype),
            kept,
            kept,
            pltpu.SemaphoreType.DMA((frames, PARTS)),
        ],
        compiler_params=pltpu.CompilerParams(vmem_limit_bytes=51 << 20),
        name="score",
    )(own, other, features.reshape(frames, rows_here, W, chan))


def merge_kernel(pixels, parts_ref, inputs_ref, far_ref, near_ref):
    tiles, frames = parts_ref.shape[1], parts_ref.shape[2]
    frame_idx, last = lax.axis_index("frame"), lax.axis_size("frame") - 1
    even = 1 - frame_idx % 2

    def joined(side, f):
        parts = [parts_ref[side, k, f] for k in range(tiles)]
        peak = functools.reduce(jnp.maximum, [p[0:1] for p in parts])
        sums = functools.reduce(jnp.add, [p[1:4] * jnp.exp(p[0:1] - peak) for p in parts])
        total = sums[0:1]
        log_total = jnp.log(total)
        return jnp.concatenate(
            [sums[1:2] / total, sums[2:3] / total, -log_total, peak + log_total - math.log(pixels)], axis=0
        )

    for f in range(frames):
        inputs_ref[f] = joined(even, f)
    far = joined(1 - even, even * (frames - 1))
    outside = (frame_idx == 0) | (frame_idx == last)
    far_ref[...] = jnp.where(outside, 0.0, far)
    near_ref[...] = jnp.where(even == 1, inputs_ref[frames - 1], inputs_ref[0])


def merge(parts, pixels):
    _, _, frames, stats, share = parts.shape
    vmem = pl.BlockSpec(memory_space=pltpu.VMEM)
    edge = jax.ShapeDtypeStruct((stats, share), jnp.float32)
    return pl.pallas_call(
        functools.partial(merge_kernel, pixels),
        out_shape=(jax.ShapeDtypeStruct((frames, stats, share), jnp.float32), edge, edge),
        in_specs=[vmem],
        out_specs=(vmem, vmem, vmem),
        compiler_params=pltpu.CompilerParams(vmem_limit_bytes=4 << 20),
        name="merge",
    )(parts)


def split(array, count):
    parts = []
    for _ in range(count):
        parts.append(array.astype(jnp.bfloat16))
        array = array - parts[-1].astype(jnp.float32)
    return parts


MEET = ((0, 0), (0, 1), (1, 0), (1, 1), (0, 2), (2, 0))
DEPTH = 128


def prepare_kernel(weight_ref, bias_ref, out_weight_ref, taps_ref, last_ref):
    taps, stats, hidden = weight_ref.shape
    rows = jnp.concatenate([weight_ref[k] for k in range(taps)] + [jnp.broadcast_to(bias_ref[...], (4, hidden))], axis=0)
    thirds = [p.astype(jnp.float32) for p in split(rows, 3)]
    stacked = jnp.concatenate([thirds[i] for i, _ in MEET], axis=0)
    filler = jnp.zeros((DEPTH - stacked.shape[0], hidden), jnp.float32)
    taps_ref[...] = jnp.transpose(jnp.concatenate([stacked, filler], axis=0)).astype(jnp.bfloat16)
    thirds = [p.astype(jnp.float32) for p in split(out_weight_ref[...], 2)]
    filler = jnp.zeros((8 - out_weight_ref.shape[0], hidden), jnp.float32)
    last_ref[...] = jnp.concatenate([thirds[0], filler, thirds[1], filler], axis=0).astype(jnp.bfloat16)


def prepare(conv_weight, conv_bias, out_weight):
    hidden = conv_bias.shape[0]
    vmem = pl.BlockSpec(memory_space=pltpu.VMEM)
    return pl.pallas_call(
        prepare_kernel,
        out_shape=(
            jax.ShapeDtypeStruct((hidden, DEPTH), jnp.bfloat16),
            jax.ShapeDtypeStruct((16, hidden), jnp.bfloat16),
        ),
        in_specs=[vmem] * 3,
        out_specs=(vmem, vmem),
        cost_estimate=pl.CostEstimate(flops=200000, bytes_accessed=200000, transcendentals=0),
        compiler_params=pltpu.CompilerParams(vmem_limit_bytes=8 << 20),
        name="prepare",
    )(conv_weight, conv_bias[None, :], out_weight)


def refine_kernel(far_ref, inputs_ref, near_ref, taps_ref, last_ref, out_ref, held, sem):
    frames, share = inputs_ref.shape[0], inputs_ref.shape[2]
    odd = lax.axis_index("frame") % 2 == 1
    far, near = far_ref[...], near_ref[...]
    before, after = jnp.where(odd, near, far), jnp.where(odd, far, near)
    line = [before] + [inputs_ref[f] for f in range(frames)] + [after]
    unit = jnp.where(lax.broadcasted_iota(jnp.int32, (4, share), 0) == 0, 1.0, 0.0)
    right = []
    for f in range(frames):
        rows = jnp.concatenate([line[f + k] for k in range(3)] + [unit], axis=0)
        thirds = [p.astype(jnp.float32) for p in split(rows, 3)]
        stacked = jnp.concatenate([thirds[j] for _, j in MEET], axis=0)
        filler = jnp.zeros((DEPTH - stacked.shape[0], share), jnp.float32)
        right.append(jnp.concatenate([stacked, filler], axis=0).astype(jnp.bfloat16))
    for f in range(frames):
        acc = jnp.dot(taps_ref[...], right[f], preferred_element_type=jnp.float32)
        hidden = jax.nn.gelu(acc)
        high, rest = split(hidden, 2)
        first = jnp.dot(last_ref[...], high, preferred_element_type=jnp.float32)
        second = jnp.dot(last_ref[...], rest, preferred_element_type=jnp.float32)
        delta = first[0:3] + (first[8:11] + second[0:3])
        moved = line[f + 1][0:3] + delta
        for o in range(3):
            held[o, f : f + 1] = moved[o : o + 1]
    store = pltpu.make_async_copy(held, out_ref, sem)
    store.start()
    store.wait()


def refine(far, inputs, near, taps, last):
    frames, _, share = inputs.shape
    moved = pl.pallas_call(
        refine_kernel,
        out_shape=jax.ShapeDtypeStruct((3, frames, share), jnp.float32),
        in_specs=[pl.BlockSpec(memory_space=pltpu.VMEM)] * 5,
        out_specs=pl.BlockSpec(memory_space=pltpu.MemorySpace.HBM),
        scratch_shapes=[pltpu.VMEM((3, frames, share), jnp.float32), pltpu.SemaphoreType.DMA],
        compiler_params=pltpu.CompilerParams(vmem_limit_bytes=8 << 20),
        name="refine",
    )(far, inputs, near, taps, last)
    return jnp.transpose(moved, (1, 0, 2))


def local(features, query_frame, query_row, query_col, conv_weight, conv_bias, out_weight):
    frame_count, pix_count, chan = features.shape
    rows_here = pix_count // W
    tiles, groups = lax.axis_size("tile"), lax.axis_size("frame")
    plane, column, couple = mesh_groups()
    keep, send = pick(features, query_frame, query_row, query_col, rows_here)
    swap = [(i, i ^ 1) for i in range(tiles)]
    mine = keep + lax.ppermute(send, "tile", swap)
    wide, tall = len(plane[0]), len(column[0])
    rows = mine.shape[0] // wide
    got = lax.all_to_all(mine.reshape(wide, rows, chan), "frame", 0, 0, axis_index_groups=plane)
    piece = jnp.sum(got, axis=0)
    got = lax.all_to_all(jnp.broadcast_to(piece, (tall, rows, chan)), BOTH, 0, 0, axis_index_groups=column)
    piece = jnp.sum(got, axis=0)
    got = lax.all_to_all(jnp.broadcast_to(piece, (wide, rows, chan)), "frame", 0, 0, axis_index_groups=plane)
    own = got.reshape(wide * rows, chan)
    other = lax.ppermute(own, "tile", swap)
    parts = score(own, other, features, rows_here)
    members = 2 * tiles
    shape = parts.shape
    parts = lax.all_to_all(parts.reshape(members, *shape[2:]), BOTH, 0, 0, axis_index_groups=couple)
    inputs, far, near = merge(parts.reshape(shape), rows_here * tiles * W)
    near = lax.ppermute(near, "frame", [(i, i ^ 1) for i in range(groups)])
    taps, last_weight = prepare(conv_weight, conv_bias, out_weight)
    return refine(far, inputs, near, taps, last_weight)


def solution(mesh):
    in_specs = (P("frame", "tile", None), P(), P(), P(), P(), P(), P())
    out_specs = P("frame", None, "tile")
    return jax.shard_map(local, mesh=mesh, in_specs=in_specs, out_specs=out_specs, check_vma=False)
```

```python
import functools
import math

import jax
import jax.numpy as jnp
from jax import lax
from jax.experimental import pallas as pl
from jax.experimental.pallas import tpu as pltpu
from jax.sharding import PartitionSpec as P

W = 480
LOG2E = math.log2(math.e)
BOTH = ("frame", "tile")


def mesh_groups():
    plane = [[x * 8 + zh * 4 + y for x in range(4) for y in range(4)] for zh in range(2)]
    column = [
        [(x * 8 + zh * 4 + y) * 8 + zl * 2 + c for zh in range(2) for zl in range(4)]
        for x in range(4)
        for y in range(4)
        for c in range(2)
    ]
    tower = [[(x * 8 + zh * 4 + y) * 8 + t for zh in range(2) for t in range(8)] for x in range(4) for y in range(4)]
    return plane, column, tower


def far_pairs():
    pairs = []
    for i in range(32):
        x, zh, y = i // 8, i // 4 % 2, i % 4
        if y in (1, 2):
            pairs.append((i, i + 1 if y == 1 else i - 1))
        elif y == 3 and (zh == 1 or x < 3):
            pairs.append((i, (x + 1 - zh) * 8 + zh * 4))
        elif y == 0 and (zh == 0 or x > 0):
            pairs.append((i, (x - zh) * 8 + zh * 4 + 3))
    return pairs


BATCH = 4


def pick_kernel(rows_here, idx_ref, feat_ref, keep_ref, send_ref, vm, sm, found_at, slots, wide, lines, sems, sem):
    frame_idx, tile_idx = lax.axis_index("frame"), lax.axis_index("tile")
    core = tile_idx % 2
    pix_count = rows_here * W
    frame_count = feat_ref.shape[0] // pix_count
    half = keep_ref.shape[0]
    sets, groups = idx_ref.shape
    lines[...] = jnp.zeros_like(lines)
    frame = jnp.right_shift(idx_ref[...], 18) - frame_idx * frame_count
    row = (jnp.right_shift(idx_ref[...], 9) & 511) - tile_idx * rows_here
    owned = (frame >= 0) & (frame < frame_count) & (row >= 0) & (row < rows_here)
    vm[0:sets, :] = frame * pix_count + row * W + (idx_ref[...] & 511)
    bit = lax.broadcasted_iota(jnp.int32, owned.shape, 0)
    word = jnp.sum(jnp.where(owned, jnp.left_shift(1, bit), 0), axis=0, keepdims=True)
    word = word | jnp.left_shift(pltpu.roll(word, groups // 2, axis=1), sets)
    vm[sets : sets + 8, :] = jnp.broadcast_to(word, (8, groups))
    to_scalar = pltpu.make_async_copy(vm, sm, sems)
    to_scalar.start()
    to_scalar.wait()

    def copy(k, pix):
        first = pl.multiple_of(pix & ~15, 16)
        return pltpu.make_async_copy(
            feat_ref.at[pl.ds(first, 16), :], slots.at[pl.ds(pl.multiple_of(k * 16, 16), 16), :], sem
        )

    def group(g, count):
        def step(state):
            left, count = state
            i = 31 - lax.clz(left & -left)
            at, lane = i & (sets - 1), g + lax.shift_right_logical(i, sets.bit_length() - 1) * (groups // 2)
            pix = sm[at, lane]
            copy(count, pix).start()
            found_at[0, count] = at * groups + lane
            found_at[1, count] = pix & 15
            return left & (left - 1), count + 1

        return lax.while_loop(lambda state: state[0] != 0, step, (sm[sets, g], count))[1]

    found = lax.fori_loop(0, groups // 2, group, 0)
    for k in range(BATCH - 1):
        found_at[0, found + k] = lines.shape[0] - 8
        found_at[1, found + k] = 0

    def wait(rows):
        def step(k, carry):
            pltpu.make_async_copy(feat_ref.at[pl.ds(0, rows), :], slots.at[pl.ds(0, rows), :], sem).wait()
            return carry

        return step

    lax.fori_loop(0, lax.shift_right_logical(found, 3), wait(128), 0)
    lax.fori_loop(0, found & 7, wait(16), 0)

    def place(batch, carry):
        for k in range(BATCH):
            at = pl.multiple_of((batch * BATCH + k) * 16, 16)
            wide[k] = slots[pl.ds(at, 16), :].astype(jnp.float32)
        picked = [wide[k, pl.ds(found_at[1, batch * BATCH + k], 1), :] for k in range(BATCH)]
        for k in range(BATCH):
            lines[pl.ds(found_at[0, batch * BATCH + k], 1), :] = picked[k]
        return carry

    lax.fori_loop(0, lax.div(found + BATCH - 1, BATCH), place, 0)
    mine = pl.multiple_of(core * half, half)
    theirs = pl.multiple_of((1 - core) * half, half)
    keep_ref[...] = (lines[pl.ds(mine, half), :] * 0.0625).astype(keep_ref.dtype)
    send_ref[...] = (lines[pl.ds(theirs, half), :] * 0.0625).astype(send_ref.dtype)


def pick(features, query_frame, query_row, query_col, rows_here):
    flat = features.reshape(-1, features.shape[2])
    queries, chan = query_frame.shape[0], features.shape[2]
    lanes = 128
    sets = queries // lanes
    half = jax.ShapeDtypeStruct((queries // 2, chan), features.dtype)
    vmem = pl.BlockSpec(memory_space=pltpu.VMEM)
    hbm = pl.BlockSpec(memory_space=pltpu.MemorySpace.HBM)
    return pl.pallas_call(
        functools.partial(pick_kernel, rows_here),
        out_shape=(half, half),
        in_specs=[vmem, hbm],
        out_specs=(vmem, vmem),
        scratch_shapes=[
            pltpu.VMEM((sets + 8, lanes), jnp.int32),
            pltpu.SMEM((sets + 8, lanes), jnp.int32),
            pltpu.SMEM((2, queries + BATCH), jnp.int32),
            pltpu.VMEM(((queries + BATCH) * 16, chan), features.dtype),
            pltpu.VMEM((BATCH, 16, chan), jnp.float32),
            pltpu.VMEM((queries + 8, chan), jnp.float32),
            pltpu.SemaphoreType.DMA,
            pltpu.SemaphoreType.DMA,
        ],
        compiler_params=pltpu.CompilerParams(vmem_limit_bytes=51 << 20),
        name="pick",
    )((query_frame * 2**18 + query_row * 2**9 + query_col).reshape(sets, lanes), flat)


BLOCK = 256
PARTS = 5
UNITS = 2


def score_kernel(own_ref, other_ref, feat_ref, out_ref, fbuf, even, odd, sems):
    tile_idx = lax.axis_index("tile")
    core = tile_idx % 2
    frames, rows_here = fbuf.shape[0], fbuf.shape[1]
    cols = W // PARTS
    loads = [
        [
            pltpu.make_async_copy(
                feat_ref.at[f, :, pl.ds(i * cols, cols), :], fbuf.at[f, :, pl.ds(i * cols, cols), :], sems.at[f, i]
            )
            for i in range(PARTS)
        ]
        for f in range(frames)
    ]
    for load in loads[0] + loads[1]:
        load.start()
    half_blocks = own_ref.shape[0] // BLOCK
    blocks = 2 * half_blocks
    pairs = blocks // UNITS
    steps = frames * pairs
    total_rows = float(rows_here * lax.axis_size("tile"))
    first_row = (tile_idx * rows_here).astype(jnp.float32)
    sub = lax.broadcasted_iota(jnp.int32, (8, BLOCK), 0).astype(jnp.float32)
    zero = jnp.zeros((8, BLOCK), jnp.float32)
    low = jnp.full((8, BLOCK), -jnp.inf, jnp.float32)

    def stage(pair):
        for m in range(UNITS):
            ref, k = (own_ref, pair * UNITS + m) if pair * UNITS < half_blocks else (other_ref, pair * UNITS + m - half_blocks)
            pltpu.matmul_push_rhs(ref[k * BLOCK : (k + 1) * BLOCK, :], 0, m, transpose=True)

    def run(*accs):
        def moves(f, part, staged, kept, was, tops):
            for r in range(rows_here):
                seen = None if tops is None else []
                if tops is not None:
                    for m in range(UNITS):
                        scores = pltpu.matmul_pop(accs[m * rows_here + r])
                        kept[was, m, r * cols : (r + 1) * cols, :] = scores
                        tops[m] = jnp.maximum(tops[m], jnp.max(scores.reshape(cols // 8, 8, BLOCK), axis=0))
                        seen.append(scores[cols - 8 : cols, :])
                if f is not None:
                    lhs = fbuf[f, r, pl.ds(pl.multiple_of(part * cols, 16), cols), :]
                    for m in range(UNITS):
                        pltpu.matmul_acc_lhs(accs[m * rows_here + r], lhs, load_staged_rhs=staged if r == 0 else None)
                yield seen

        def weighs(kept, part, peaks, sums):
            start = jnp.asarray(part * cols).astype(jnp.float32)
            here, across = [None] * UNITS, [None] * UNITS
            for k in range(cols // 8):
                for m in range(UNITS):
                    tail, below = None, None
                    for r in reversed(range(rows_here)):
                        at = r * cols + k * 8
                        expo = jnp.exp2((kept[part, m, at : at + 8, :] - peaks[m]) * LOG2E)
                        tail = expo if tail is None else tail + expo
                        if r > 0:
                            below = tail if below is None else below + tail
                    sums[m][2] = sums[m][2] + below
                    here[m] = tail if here[m] is None else here[m] + tail
                    if k > 0:
                        shifted = tail * float(k * 8)
                        across[m] = shifted if across[m] is None else across[m] + shifted
                    yield
            for m in range(UNITS):
                sums[m][0] = sums[m][0] + here[m]
                sums[m][1] = sums[m][1] + (across[m] + here[m] * (sub + start))

        def weave(moving, weighing, peaks):
            per = (cols // 8) * UNITS // rows_here
            if moving is None:
                moving = iter(())
            if weighing is None:
                weighing = iter(())
            for _ in range(rows_here):
                seen = next(moving, None)
                if seen is not None and peaks is not None:
                    for m in range(UNITS):
                        peaks[m] = jnp.minimum(peaks[m], jnp.maximum(peaks[m], seen[m]))
                for _ in range(per):
                    next(weighing, None)
            for _ in moving:
                pass
            for _ in weighing:
                pass

        def settle(tops):
            return tuple(jnp.broadcast_to(jnp.max(t, axis=0, keepdims=True), t.shape) for t in tops)

        def finish(step, peaks, sums):
            f, pair = divmod(step, pairs)
            for m in range(UNITS):
                total, sum_x, sum_y = [jnp.sum(a, axis=0, keepdims=True) for a in sums[m]]
                where_to = lax.rem(pair * UNITS + m + core * half_blocks, blocks)
                packed = jnp.concatenate(
                    [peaks[m][0:1], total, sum_x * (1.0 / W), (sum_y + first_row * total) * (1.0 / total_rows)], axis=0
                )
                for side in range(2):
                    out_ref[side, where_to, f] = packed

        none, fresh = (low,) * UNITS, ((zero, zero, zero),) * UNITS
        stage(0)
        loads[0][0].wait()
        tops, peaks, sums = None, None, None
        for step in range(steps + 2):
            f = step // pairs if step < steps else None
            new, old = (even, odd) if step % 2 == 0 else (odd, even)
            if step == pairs:
                for load in loads[1]:
                    load.wait()
            last_peaks = peaks
            tops = None if tops is None else list(tops)
            sums = None if sums is None else [list(x) for x in sums]
            bound = None if last_peaks is None else list(last_peaks)
            weave(
                moves(f, 0, 0, old, PARTS - 1, tops) if step <= steps else None,
                weighs(new, PARTS - 1, bound, sums) if step > 1 else None,
                bound,
            )
            if step <= steps:
                peaks = None if tops is None else settle(tops)
            if step + 1 < steps:
                stage((step + 1) % pairs)
            if step > 1:
                finish(step - 2, last_peaks, sums)
            if step > steps:
                break

            def part_of(i, state):
                tops, sums = state
                if step == 0:
                    pltpu.make_async_copy(
                        feat_ref.at[0, :, pl.ds(0, cols), :], fbuf.at[0, :, pl.ds(0, cols), :], sems.at[0, i]
                    ).wait()
                tops, sums = list(tops), [list(x) for x in sums]
                bound = None if peaks is None else list(peaks)
                weave(
                    moves(f, i, None, new, i - 1, tops) if step < steps else None,
                    weighs(old, i - 1, bound, sums) if step > 0 else None,
                    bound,
                )
                tops, sums = tuple(tops), tuple(tuple(x) for x in sums)
                return tops, sums

            tops, sums = lax.fori_loop(1, PARTS, part_of, (none, fresh))

    pl.run_scoped(
        run, *[pltpu.ACC(m)((cols, BLOCK), jnp.float32) for m in range(UNITS) for _ in range(rows_here)]
    )


def score(own, other, features, rows_here):
    frames, pix_count, chan = features.shape
    blocks = 2 * own.shape[0] // BLOCK
    vmem = pl.BlockSpec(memory_space=pltpu.VMEM)
    kept = pltpu.VMEM((PARTS, UNITS, pix_count // PARTS, BLOCK), jnp.float32)
    return pl.pallas_call(
        score_kernel,
        out_shape=jax.ShapeDtypeStruct((2, blocks, frames, 4, BLOCK), jnp.float32),
        in_specs=[vmem, vmem, pl.BlockSpec(memory_space=pltpu.MemorySpace.HBM)],
        out_specs=vmem,
        scratch_shapes=[
            pltpu.VMEM((frames, rows_here, W, chan), features.dtype),
            kept,
            kept,
            pltpu.SemaphoreType.DMA((frames, PARTS)),
        ],
        compiler_params=pltpu.CompilerParams(vmem_limit_bytes=51 << 20),
        name="score",
    )(own, other, features.reshape(frames, rows_here, W, chan))


def merge_kernel(pixels, parts_ref, inputs_ref, far_ref, near_ref):
    tiles, frames = parts_ref.shape[1], parts_ref.shape[2]
    frame_idx = lax.axis_index("frame")
    here, y = frame_idx // 4 % 2, frame_idx % 4
    odd = y % 2

    def joined(side, f):
        parts = [parts_ref[side, k, f] for k in range(tiles)]
        peak = functools.reduce(jnp.maximum, [p[0:1] for p in parts])
        sums = functools.reduce(jnp.add, [p[1:4] * jnp.exp(p[0:1] - peak) for p in parts])
        total = sums[0:1]
        log_total = jnp.log(total)
        return jnp.concatenate(
            [sums[1:2] / total, sums[2:3] / total, -log_total, peak + log_total - math.log(pixels)], axis=0
        )

    for f in range(frames):
        inputs_ref[f] = joined(here, f)
    across = joined(1 - here, odd * (frames - 1))
    first, last = inputs_ref[0], inputs_ref[frames - 1]
    far_ref[...] = jnp.where((y == 0) | (y == 3), across, jnp.where(odd == 1, last, first))
    near_ref[...] = jnp.where(odd == 1, first, last)


def merge(parts, pixels):
    _, _, frames, stats, share = parts.shape
    vmem = pl.BlockSpec(memory_space=pltpu.VMEM)
    edge = jax.ShapeDtypeStruct((stats, share), jnp.float32)
    return pl.pallas_call(
        functools.partial(merge_kernel, pixels),
        out_shape=(jax.ShapeDtypeStruct((frames, stats, share), jnp.float32), edge, edge),
        in_specs=[vmem],
        out_specs=(vmem, vmem, vmem),
        compiler_params=pltpu.CompilerParams(vmem_limit_bytes=4 << 20),
        name="merge",
    )(parts)


def split(array, count):
    parts = []
    for _ in range(count):
        parts.append(array.astype(jnp.bfloat16))
        array = array - parts[-1].astype(jnp.float32)
    return parts


MEET = ((0, 0), (0, 1), (1, 0), (1, 1), (0, 2), (2, 0))
DEPTH = 128


def prepare_kernel(weight_ref, bias_ref, out_weight_ref, taps_ref, last_ref):
    taps, stats, hidden = weight_ref.shape
    rows = jnp.concatenate([weight_ref[k] for k in range(taps)] + [jnp.broadcast_to(bias_ref[...], (4, hidden))], axis=0)
    thirds = [p.astype(jnp.float32) for p in split(rows, 3)]
    stacked = jnp.concatenate([thirds[i] for i, _ in MEET], axis=0)
    filler = jnp.zeros((DEPTH - stacked.shape[0], hidden), jnp.float32)
    taps_ref[...] = jnp.transpose(jnp.concatenate([stacked, filler], axis=0)).astype(jnp.bfloat16)
    thirds = [p.astype(jnp.float32) for p in split(out_weight_ref[...], 2)]
    filler = jnp.zeros((8 - out_weight_ref.shape[0], hidden), jnp.float32)
    last_ref[...] = jnp.concatenate([thirds[0], filler, thirds[1], filler], axis=0).astype(jnp.bfloat16)


def prepare(conv_weight, conv_bias, out_weight):
    hidden = conv_bias.shape[0]
    vmem = pl.BlockSpec(memory_space=pltpu.VMEM)
    return pl.pallas_call(
        prepare_kernel,
        out_shape=(
            jax.ShapeDtypeStruct((hidden, DEPTH), jnp.bfloat16),
            jax.ShapeDtypeStruct((16, hidden), jnp.bfloat16),
        ),
        in_specs=[vmem] * 3,
        out_specs=(vmem, vmem),
        cost_estimate=pl.CostEstimate(flops=200000, bytes_accessed=200000, transcendentals=0),
        compiler_params=pltpu.CompilerParams(vmem_limit_bytes=8 << 20),
        name="prepare",
    )(conv_weight, conv_bias[None, :], out_weight)


def refine_kernel(far_ref, inputs_ref, near_ref, taps_ref, last_ref, out_ref, held, sem):
    frames, share = inputs_ref.shape[0], inputs_ref.shape[2]
    odd = lax.axis_index("frame") % 2 == 1
    far, near = far_ref[...], near_ref[...]
    before, after = jnp.where(odd, near, far), jnp.where(odd, far, near)
    line = [before] + [inputs_ref[f] for f in range(frames)] + [after]
    unit = jnp.where(lax.broadcasted_iota(jnp.int32, (4, share), 0) == 0, 1.0, 0.0)
    right = []
    for f in range(frames):
        rows = jnp.concatenate([line[f + k] for k in range(3)] + [unit], axis=0)
        thirds = [p.astype(jnp.float32) for p in split(rows, 3)]
        stacked = jnp.concatenate([thirds[j] for _, j in MEET], axis=0)
        filler = jnp.zeros((DEPTH - stacked.shape[0], share), jnp.float32)
        right.append(jnp.concatenate([stacked, filler], axis=0).astype(jnp.bfloat16))
    for f in range(frames):
        acc = jnp.dot(taps_ref[...], right[f], preferred_element_type=jnp.float32)
        hidden = jax.nn.gelu(acc)
        high, rest = split(hidden, 2)
        first = jnp.dot(last_ref[...], high, preferred_element_type=jnp.float32)
        second = jnp.dot(last_ref[...], rest, preferred_element_type=jnp.float32)
        delta = first[0:3] + (first[8:11] + second[0:3])
        moved = line[f + 1][0:3] + delta
        for o in range(3):
            held[o, f : f + 1] = moved[o : o + 1]
    store = pltpu.make_async_copy(held, out_ref, sem)
    store.start()
    store.wait()


def refine(far, inputs, near, taps, last):
    frames, _, share = inputs.shape
    moved = pl.pallas_call(
        refine_kernel,
        out_shape=jax.ShapeDtypeStruct((3, frames, share), jnp.float32),
        in_specs=[pl.BlockSpec(memory_space=pltpu.VMEM)] * 5,
        out_specs=pl.BlockSpec(memory_space=pltpu.MemorySpace.HBM),
        scratch_shapes=[pltpu.VMEM((3, frames, share), jnp.float32), pltpu.SemaphoreType.DMA],
        compiler_params=pltpu.CompilerParams(vmem_limit_bytes=8 << 20),
        name="refine",
    )(far, inputs, near, taps, last)
    return jnp.transpose(moved, (1, 0, 2))


def local(features, query_frame, query_row, query_col, conv_weight, conv_bias, out_weight):
    frame_count, pix_count, chan = features.shape
    rows_here = pix_count // W
    tiles, groups = lax.axis_size("tile"), lax.axis_size("frame")
    plane, column, tower = mesh_groups()
    keep, send = pick(features, query_frame, query_row, query_col, rows_here)
    swap = [(i, i ^ 1) for i in range(tiles)]
    mine = keep + lax.ppermute(send, "tile", swap)
    wide, tall = len(plane[0]), len(column[0])
    rows = mine.shape[0] // wide
    got = lax.all_to_all(mine.reshape(wide, rows, chan), "frame", 0, 0, axis_index_groups=plane)
    piece = jnp.sum(got, axis=0)
    got = lax.all_to_all(jnp.broadcast_to(piece, (tall, rows, chan)), BOTH, 0, 0, axis_index_groups=column)
    piece = jnp.sum(got, axis=0)
    got = lax.all_to_all(jnp.broadcast_to(piece, (wide, rows, chan)), "frame", 0, 0, axis_index_groups=plane)
    own = got.reshape(wide * rows, chan)
    other = lax.ppermute(own, "tile", swap)
    parts = score(own, other, features, rows_here)
    members = 2 * tiles
    shape = parts.shape
    parts = lax.all_to_all(parts.reshape(members, *shape[2:]), BOTH, 0, 0, axis_index_groups=tower)
    inputs, far, near = merge(parts.reshape(shape), rows_here * tiles * W)
    far = lax.ppermute(far, "frame", far_pairs())
    near = lax.ppermute(near, "frame", [(i, i ^ 1) for i in range(groups)])
    taps, last_weight = prepare(conv_weight, conv_bias, out_weight)
    return refine(far, inputs, near, taps, last_weight)


def solution(mesh):
    in_specs = (P("frame", "tile", None), P(), P(), P(), P(), P(), P())
    out_specs = P("frame", None, "tile")
    return jax.shard_map(local, mesh=mesh, in_specs=in_specs, out_specs=out_specs, check_vma=False)
```

```python
import functools
import math

import jax
import jax.numpy as jnp
from jax import lax
from jax.experimental import pallas as pl
from jax.experimental.pallas import tpu as pltpu
from jax.sharding import PartitionSpec as P

W = 480
LOG2E = math.log2(math.e)
BOTH = ("frame", "tile")


def mesh_groups():
    plane = [[x * 8 + zh * 4 + y for x in range(4) for y in range(4)] for zh in range(2)]
    column = [
        [(x * 8 + zh * 4 + y) * 8 + zl * 2 + c for zh in range(2) for zl in range(4)]
        for x in range(4)
        for y in range(4)
        for c in range(2)
    ]
    tower = [[(x * 8 + zh * 4 + y) * 8 + t for zh in range(2) for t in range(8)] for x in range(4) for y in range(4)]
    return plane, column, tower


def far_pairs():
    pairs = []
    for i in range(32):
        x, zh, y = i // 8, i // 4 % 2, i % 4
        if y in (1, 2):
            pairs.append((i, i + 1 if y == 1 else i - 1))
        elif y == 3 and (zh == 1 or x < 3):
            pairs.append((i, (x + 1 - zh) * 8 + zh * 4))
        elif y == 0 and (zh == 0 or x > 0):
            pairs.append((i, (x - zh) * 8 + zh * 4 + 3))
    return pairs


BATCH = 4


def pick_kernel(rows_here, idx_ref, feat_ref, keep_ref, send_ref, vm, sm, found_at, slots, wide, lines, sems, sem):
    frame_idx, tile_idx = lax.axis_index("frame"), lax.axis_index("tile")
    core = tile_idx % 2
    pix_count = rows_here * W
    frame_count = feat_ref.shape[0] // pix_count
    half = keep_ref.shape[0]
    sets, groups = idx_ref.shape
    lines[...] = jnp.zeros_like(lines)
    frame = jnp.right_shift(idx_ref[...], 18) - frame_idx * frame_count
    row = (jnp.right_shift(idx_ref[...], 9) & 511) - tile_idx * rows_here
    owned = (frame >= 0) & (frame < frame_count) & (row >= 0) & (row < rows_here)
    vm[0:sets, :] = frame * pix_count + row * W + (idx_ref[...] & 511)
    bit = lax.broadcasted_iota(jnp.int32, owned.shape, 0)
    word = jnp.sum(jnp.where(owned, jnp.left_shift(1, bit), 0), axis=0, keepdims=True)
    word = word | jnp.left_shift(pltpu.roll(word, groups // 2, axis=1), sets)
    vm[sets : sets + 8, :] = jnp.broadcast_to(word, (8, groups))
    to_scalar = pltpu.make_async_copy(vm, sm, sems)
    to_scalar.start()
    to_scalar.wait()

    def copy(k, pix):
        first = pl.multiple_of(pix & ~15, 16)
        return pltpu.make_async_copy(
            feat_ref.at[pl.ds(first, 16), :], slots.at[pl.ds(pl.multiple_of(k * 16, 16), 16), :], sem
        )

    def group(g, count):
        def step(state):
            left, count = state
            i = 31 - lax.clz(left & -left)
            at, lane = i & (sets - 1), g + lax.shift_right_logical(i, sets.bit_length() - 1) * (groups // 2)
            pix = sm[at, lane]
            copy(count, pix).start()
            found_at[0, count] = at * groups + lane
            found_at[1, count] = pix & 15
            return left & (left - 1), count + 1

        return lax.while_loop(lambda state: state[0] != 0, step, (sm[sets, g], count))[1]

    found = lax.fori_loop(0, groups // 2, group, 0)
    for k in range(BATCH - 1):
        found_at[0, found + k] = lines.shape[0] - 8
        found_at[1, found + k] = 0

    def wait(rows):
        def step(k, carry):
            pltpu.make_async_copy(feat_ref.at[pl.ds(0, rows), :], slots.at[pl.ds(0, rows), :], sem).wait()
            return carry

        return step

    lax.fori_loop(0, lax.shift_right_logical(found, 3), wait(128), 0)
    lax.fori_loop(0, found & 7, wait(16), 0)

    def place(batch, carry):
        for k in range(BATCH):
            at = pl.multiple_of((batch * BATCH + k) * 16, 16)
            wide[k] = slots[pl.ds(at, 16), :].astype(jnp.float32)
        picked = [wide[k, pl.ds(found_at[1, batch * BATCH + k], 1), :] for k in range(BATCH)]
        for k in range(BATCH):
            lines[pl.ds(found_at[0, batch * BATCH + k], 1), :] = picked[k]
        return carry

    lax.fori_loop(0, lax.div(found + BATCH - 1, BATCH), place, 0)
    mine = pl.multiple_of(core * half, half)
    theirs = pl.multiple_of((1 - core) * half, half)
    keep_ref[...] = (lines[pl.ds(mine, half), :] * 0.0625).astype(keep_ref.dtype)
    send_ref[...] = (lines[pl.ds(theirs, half), :] * 0.0625).astype(send_ref.dtype)


def pick(features, query_frame, query_row, query_col, rows_here):
    flat = features.reshape(-1, features.shape[2])
    queries, chan = query_frame.shape[0], features.shape[2]
    lanes = 128
    sets = queries // lanes
    half = jax.ShapeDtypeStruct((queries // 2, chan), features.dtype)
    vmem = pl.BlockSpec(memory_space=pltpu.VMEM)
    hbm = pl.BlockSpec(memory_space=pltpu.MemorySpace.HBM)
    return pl.pallas_call(
        functools.partial(pick_kernel, rows_here),
        out_shape=(half, half),
        in_specs=[vmem, hbm],
        out_specs=(vmem, vmem),
        scratch_shapes=[
            pltpu.VMEM((sets + 8, lanes), jnp.int32),
            pltpu.SMEM((sets + 8, lanes), jnp.int32),
            pltpu.SMEM((2, queries + BATCH), jnp.int32),
            pltpu.VMEM(((queries + BATCH) * 16, chan), features.dtype),
            pltpu.VMEM((BATCH, 16, chan), jnp.float32),
            pltpu.VMEM((queries + 8, chan), jnp.float32),
            pltpu.SemaphoreType.DMA,
            pltpu.SemaphoreType.DMA,
        ],
        compiler_params=pltpu.CompilerParams(vmem_limit_bytes=51 << 20),
        name="pick",
    )((query_frame * 2**18 + query_row * 2**9 + query_col).reshape(sets, lanes), flat)


BLOCK = 256
PARTS = 5
UNITS = 2


def score_kernel(own_ref, other_ref, fbuf, out_ref, even, odd):
    tile_idx = lax.axis_index("tile")
    core = tile_idx % 2
    frames, rows_here = fbuf.shape[0], fbuf.shape[1]
    cols = W // PARTS
    half_blocks = own_ref.shape[0] // BLOCK
    blocks = 2 * half_blocks
    pairs = blocks // UNITS
    steps = frames * pairs
    total_rows = float(rows_here * lax.axis_size("tile"))
    first_row = (tile_idx * rows_here).astype(jnp.float32)
    sub = lax.broadcasted_iota(jnp.int32, (8, BLOCK), 0).astype(jnp.float32)
    zero = jnp.zeros((8, BLOCK), jnp.float32)
    low = jnp.full((8, BLOCK), -jnp.inf, jnp.float32)

    def stage(pair):
        for m in range(UNITS):
            ref, k = (own_ref, pair * UNITS + m) if pair * UNITS < half_blocks else (other_ref, pair * UNITS + m - half_blocks)
            pltpu.matmul_push_rhs(ref[k * BLOCK : (k + 1) * BLOCK, :], 0, m, transpose=True)

    def run(*accs):
        def moves(f, part, staged, kept, was, tops):
            for r in range(rows_here):
                seen = None if tops is None else []
                if tops is not None:
                    for m in range(UNITS):
                        scores = pltpu.matmul_pop(accs[m * rows_here + r])
                        kept[was, m, r * cols : (r + 1) * cols, :] = scores
                        tops[m] = jnp.maximum(tops[m], jnp.max(scores.reshape(cols // 8, 8, BLOCK), axis=0))
                        seen.append(scores[cols - 8 : cols, :])
                if f is not None:
                    lhs = fbuf[f, r, pl.ds(pl.multiple_of(part * cols, 16), cols), :]
                    for m in range(UNITS):
                        pltpu.matmul_acc_lhs(accs[m * rows_here + r], lhs, load_staged_rhs=staged if r == 0 else None)
                yield seen

        def weighs(kept, part, peaks, sums):
            start = jnp.asarray(part * cols).astype(jnp.float32)
            here, across = [None] * UNITS, [None] * UNITS
            for k in range(cols // 8):
                for m in range(UNITS):
                    tail, below = None, None
                    for r in reversed(range(rows_here)):
                        at = r * cols + k * 8
                        expo = jnp.exp2((kept[part, m, at : at + 8, :] - peaks[m]) * LOG2E)
                        tail = expo if tail is None else tail + expo
                        if r > 0:
                            below = tail if below is None else below + tail
                    sums[m][2] = sums[m][2] + below
                    here[m] = tail if here[m] is None else here[m] + tail
                    if k > 0:
                        shifted = tail * float(k * 8)
                        across[m] = shifted if across[m] is None else across[m] + shifted
                    yield
            for m in range(UNITS):
                sums[m][0] = sums[m][0] + here[m]
                sums[m][1] = sums[m][1] + (across[m] + here[m] * (sub + start))

        def weave(moving, weighing, peaks):
            per = (cols // 8) * UNITS // rows_here
            if moving is None:
                moving = iter(())
            if weighing is None:
                weighing = iter(())
            for _ in range(rows_here):
                seen = next(moving, None)
                if seen is not None and peaks is not None:
                    for m in range(UNITS):
                        peaks[m] = jnp.minimum(peaks[m], jnp.maximum(peaks[m], seen[m]))
                for _ in range(per):
                    next(weighing, None)
            for _ in moving:
                pass
            for _ in weighing:
                pass

        def settle(tops):
            return tuple(jnp.broadcast_to(jnp.max(t, axis=0, keepdims=True), t.shape) for t in tops)

        def finish(step, peaks, sums):
            f, pair = divmod(step, pairs)
            for m in range(UNITS):
                total, sum_x, sum_y = [jnp.sum(a, axis=0, keepdims=True) for a in sums[m]]
                where_to = lax.rem(pair * UNITS + m + core * half_blocks, blocks)
                packed = jnp.concatenate(
                    [peaks[m][0:1], total, sum_x * (1.0 / W), (sum_y + first_row * total) * (1.0 / total_rows)], axis=0
                )
                for side in range(2):
                    out_ref[side, where_to, f] = packed

        none, fresh = (low,) * UNITS, ((zero, zero, zero),) * UNITS
        stage(0)
        tops, peaks, sums = None, None, None
        for step in range(steps + 2):
            f = step // pairs if step < steps else None
            new, old = (even, odd) if step % 2 == 0 else (odd, even)
            last_peaks = peaks
            tops = None if tops is None else list(tops)
            sums = None if sums is None else [list(x) for x in sums]
            bound = None if last_peaks is None else list(last_peaks)
            weave(
                moves(f, 0, 0, old, PARTS - 1, tops) if step <= steps else None,
                weighs(new, PARTS - 1, bound, sums) if step > 1 else None,
                bound,
            )
            if step <= steps:
                peaks = None if tops is None else settle(tops)
            if step + 1 < steps:
                stage((step + 1) % pairs)
            if step > 1:
                finish(step - 2, last_peaks, sums)
            if step > steps:
                break

            def part_of(i, state):
                tops, sums = state
                tops, sums = list(tops), [list(x) for x in sums]
                bound = None if peaks is None else list(peaks)
                weave(
                    moves(f, i, None, new, i - 1, tops) if step < steps else None,
                    weighs(old, i - 1, bound, sums) if step > 0 else None,
                    bound,
                )
                tops, sums = tuple(tops), tuple(tuple(x) for x in sums)
                return tops, sums

            tops, sums = lax.fori_loop(1, PARTS, part_of, (none, fresh))

    pl.run_scoped(
        run, *[pltpu.ACC(m)((cols, BLOCK), jnp.float32) for m in range(UNITS) for _ in range(rows_here)]
    )


def fetch_kernel(feat_ref, own_ref, out_ref, sem):
    load = pltpu.make_async_copy(feat_ref, out_ref, sem)
    load.start()
    load.wait()


def fetch(features, own):
    hbm = pl.BlockSpec(memory_space=pltpu.MemorySpace.HBM)
    return pl.pallas_call(
        fetch_kernel,
        out_shape=jax.ShapeDtypeStruct(features.shape, features.dtype),
        in_specs=[hbm, pl.BlockSpec(memory_space=pl.ANY)],
        out_specs=pl.BlockSpec(memory_space=pltpu.VMEM),
        scratch_shapes=[pltpu.SemaphoreType.DMA],
        compiler_params=pltpu.CompilerParams(vmem_limit_bytes=47 << 20),
        cost_estimate=pl.CostEstimate(flops=0, bytes_accessed=4 << 20, transcendentals=0),
        name="fetch",
    )(features, own)


def score(own, other, features, rows_here):
    frames, pix_count, chan = features.shape
    blocks = 2 * own.shape[0] // BLOCK
    vmem = pl.BlockSpec(memory_space=pltpu.VMEM)
    kept = pltpu.VMEM((PARTS, UNITS, pix_count // PARTS, BLOCK), jnp.float32)
    return pl.pallas_call(
        score_kernel,
        out_shape=jax.ShapeDtypeStruct((2, blocks, frames, 4, BLOCK), jnp.float32),
        in_specs=[vmem, vmem, vmem],
        out_specs=vmem,
        scratch_shapes=[kept, kept],
        compiler_params=pltpu.CompilerParams(vmem_limit_bytes=24 << 20),
        name="score",
    )(own, other, features.reshape(frames, rows_here, W, chan))


def merge_kernel(pixels, parts_ref, inputs_ref, far_ref, near_ref):
    tiles, frames = parts_ref.shape[1], parts_ref.shape[2]
    frame_idx = lax.axis_index("frame")
    here, y = frame_idx // 4 % 2, frame_idx % 4
    odd = y % 2

    def joined(side, f):
        parts = [parts_ref[side, k, f] for k in range(tiles)]
        peak = functools.reduce(jnp.maximum, [p[0:1] for p in parts])
        sums = functools.reduce(jnp.add, [p[1:4] * jnp.exp(p[0:1] - peak) for p in parts])
        total = sums[0:1]
        log_total = jnp.log(total)
        return jnp.concatenate(
            [sums[1:2] / total, sums[2:3] / total, -log_total, peak + log_total - math.log(pixels)], axis=0
        )

    for f in range(frames):
        inputs_ref[f] = joined(here, f)
    across = joined(1 - here, odd * (frames - 1))
    first, last = inputs_ref[0], inputs_ref[frames - 1]
    far_ref[...] = jnp.where((y == 0) | (y == 3), across, jnp.where(odd == 1, last, first))
    near_ref[...] = jnp.where(odd == 1, first, last)


def merge(parts, pixels):
    _, _, frames, stats, share = parts.shape
    vmem = pl.BlockSpec(memory_space=pltpu.VMEM)
    edge = jax.ShapeDtypeStruct((stats, share), jnp.float32)
    return pl.pallas_call(
        functools.partial(merge_kernel, pixels),
        out_shape=(jax.ShapeDtypeStruct((frames, stats, share), jnp.float32), edge, edge),
        in_specs=[vmem],
        out_specs=(vmem, vmem, vmem),
        compiler_params=pltpu.CompilerParams(vmem_limit_bytes=4 << 20),
        name="merge",
    )(parts)


def split(array, count):
    parts = []
    for _ in range(count):
        parts.append(array.astype(jnp.bfloat16))
        array = array - parts[-1].astype(jnp.float32)
    return parts


MEET = ((0, 0), (0, 1), (1, 0), (1, 1), (0, 2), (2, 0))
DEPTH = 128


def prepare_kernel(weight_ref, bias_ref, out_weight_ref, taps_ref, last_ref):
    taps, stats, hidden = weight_ref.shape
    rows = jnp.concatenate([weight_ref[k] for k in range(taps)] + [jnp.broadcast_to(bias_ref[...], (4, hidden))], axis=0)
    thirds = [p.astype(jnp.float32) for p in split(rows, 3)]
    stacked = jnp.concatenate([thirds[i] for i, _ in MEET], axis=0)
    filler = jnp.zeros((DEPTH - stacked.shape[0], hidden), jnp.float32)
    taps_ref[...] = jnp.transpose(jnp.concatenate([stacked, filler], axis=0)).astype(jnp.bfloat16)
    thirds = [p.astype(jnp.float32) for p in split(out_weight_ref[...], 2)]
    filler = jnp.zeros((8 - out_weight_ref.shape[0], hidden), jnp.float32)
    last_ref[...] = jnp.concatenate([thirds[0], filler, thirds[1], filler], axis=0).astype(jnp.bfloat16)


def prepare(conv_weight, conv_bias, out_weight):
    hidden = conv_bias.shape[0]
    vmem = pl.BlockSpec(memory_space=pltpu.VMEM)
    return pl.pallas_call(
        prepare_kernel,
        out_shape=(
            jax.ShapeDtypeStruct((hidden, DEPTH), jnp.bfloat16),
            jax.ShapeDtypeStruct((16, hidden), jnp.bfloat16),
        ),
        in_specs=[vmem] * 3,
        out_specs=(vmem, vmem),
        cost_estimate=pl.CostEstimate(flops=200000, bytes_accessed=200000, transcendentals=0),
        compiler_params=pltpu.CompilerParams(vmem_limit_bytes=8 << 20),
        name="prepare",
    )(conv_weight, conv_bias[None, :], out_weight)


def refine_kernel(far_ref, inputs_ref, near_ref, taps_ref, last_ref, out_ref, held, sem):
    frames, share = inputs_ref.shape[0], inputs_ref.shape[2]
    odd = lax.axis_index("frame") % 2 == 1
    far, near = far_ref[...], near_ref[...]
    before, after = jnp.where(odd, near, far), jnp.where(odd, far, near)
    line = [before] + [inputs_ref[f] for f in range(frames)] + [after]
    unit = jnp.where(lax.broadcasted_iota(jnp.int32, (4, share), 0) == 0, 1.0, 0.0)
    right = []
    for f in range(frames):
        rows = jnp.concatenate([line[f + k] for k in range(3)] + [unit], axis=0)
        thirds = [p.astype(jnp.float32) for p in split(rows, 3)]
        stacked = jnp.concatenate([thirds[j] for _, j in MEET], axis=0)
        filler = jnp.zeros((DEPTH - stacked.shape[0], share), jnp.float32)
        right.append(jnp.concatenate([stacked, filler], axis=0).astype(jnp.bfloat16))
    for f in range(frames):
        acc = jnp.dot(taps_ref[...], right[f], preferred_element_type=jnp.float32)
        hidden = jax.nn.gelu(acc)
        high, rest = split(hidden, 2)
        first = jnp.dot(last_ref[...], high, preferred_element_type=jnp.float32)
        second = jnp.dot(last_ref[...], rest, preferred_element_type=jnp.float32)
        delta = first[0:3] + (first[8:11] + second[0:3])
        moved = line[f + 1][0:3] + delta
        for o in range(3):
            held[o, f : f + 1] = moved[o : o + 1]
    store = pltpu.make_async_copy(held, out_ref, sem)
    store.start()
    store.wait()


def refine(far, inputs, near, taps, last):
    frames, _, share = inputs.shape
    moved = pl.pallas_call(
        refine_kernel,
        out_shape=jax.ShapeDtypeStruct((3, frames, share), jnp.float32),
        in_specs=[pl.BlockSpec(memory_space=pltpu.VMEM)] * 5,
        out_specs=pl.BlockSpec(memory_space=pltpu.MemorySpace.HBM),
        scratch_shapes=[pltpu.VMEM((3, frames, share), jnp.float32), pltpu.SemaphoreType.DMA],
        compiler_params=pltpu.CompilerParams(vmem_limit_bytes=8 << 20),
        name="refine",
    )(far, inputs, near, taps, last)
    return jnp.transpose(moved, (1, 0, 2))


def local(features, query_frame, query_row, query_col, conv_weight, conv_bias, out_weight):
    frame_count, pix_count, chan = features.shape
    rows_here = pix_count // W
    tiles, groups = lax.axis_size("tile"), lax.axis_size("frame")
    plane, column, tower = mesh_groups()
    keep, send = pick(features, query_frame, query_row, query_col, rows_here)
    swap = [(i, i ^ 1) for i in range(tiles)]
    mine = keep + lax.ppermute(send, "tile", swap)
    wide, tall = len(plane[0]), len(column[0])
    rows = mine.shape[0] // wide
    got = lax.all_to_all(mine.reshape(wide, rows, chan), "frame", 0, 0, axis_index_groups=plane)
    piece = jnp.sum(got, axis=0)
    got = lax.all_to_all(jnp.broadcast_to(piece, (tall, rows, chan)), BOTH, 0, 0, axis_index_groups=column)
    piece = jnp.sum(got, axis=0)
    got = lax.all_to_all(jnp.broadcast_to(piece, (wide, rows, chan)), "frame", 0, 0, axis_index_groups=plane)
    own = got.reshape(wide * rows, chan)
    other = lax.ppermute(own, "tile", swap)
    parts = score(own, other, fetch(features, own), rows_here)
    members = 2 * tiles
    shape = parts.shape
    parts = lax.all_to_all(parts.reshape(members, *shape[2:]), BOTH, 0, 0, axis_index_groups=tower)
    inputs, far, near = merge(parts.reshape(shape), rows_here * tiles * W)
    far = lax.ppermute(far, "frame", far_pairs())
    near = lax.ppermute(near, "frame", [(i, i ^ 1) for i in range(groups)])
    taps, last_weight = prepare(conv_weight, conv_bias, out_weight)
    return refine(far, inputs, near, taps, last_weight)


def solution(mesh):
    in_specs = (P("frame", "tile", None), P(), P(), P(), P(), P(), P())
    out_specs = P("frame", None, "tile")
    return jax.shard_map(local, mesh=mesh, in_specs=in_specs, out_specs=out_specs, check_vma=False)
```

```python
import functools
import math

import jax
import jax.numpy as jnp
from jax import lax
from jax.experimental import pallas as pl
from jax.experimental.pallas import tpu as pltpu
from jax.sharding import PartitionSpec as P

W = 480
LOG2E = math.log2(math.e)
BOTH = ("frame", "tile")


def mesh_groups():
    plane = [[x * 8 + zh * 4 + y for x in range(4) for y in range(4)] for zh in range(2)]
    column = [
        [(x * 8 + zh * 4 + y) * 8 + zl * 2 + c for zh in range(2) for zl in range(4)]
        for x in range(4)
        for y in range(4)
        for c in range(2)
    ]
    tower = [[(x * 8 + zh * 4 + y) * 8 + t for zh in range(2) for t in range(8)] for x in range(4) for y in range(4)]
    return plane, column, tower


def far_pairs():
    pairs = []
    for i in range(32):
        x, zh, y = i // 8, i // 4 % 2, i % 4
        if y in (1, 2):
            pairs.append((i, i + 1 if y == 1 else i - 1))
        elif y == 3 and (zh == 1 or x < 3):
            pairs.append((i, (x + 1 - zh) * 8 + zh * 4))
        elif y == 0 and (zh == 0 or x > 0):
            pairs.append((i, (x - zh) * 8 + zh * 4 + 3))
    return pairs


BATCH = 4


def pick_kernel(rows_here, idx_ref, feat_ref, keep_ref, send_ref, vm, sm, found_at, slots, wide, lines, sems, sem):
    frame_idx, tile_idx = lax.axis_index("frame"), lax.axis_index("tile")
    core = tile_idx % 2
    pix_count = rows_here * W
    frame_count = feat_ref.shape[0] // pix_count
    half = keep_ref.shape[0]
    sets, groups = idx_ref.shape
    lines[...] = jnp.zeros_like(lines)
    frame = jnp.right_shift(idx_ref[...], 18) - frame_idx * frame_count
    row = (jnp.right_shift(idx_ref[...], 9) & 511) - tile_idx * rows_here
    owned = (frame >= 0) & (frame < frame_count) & (row >= 0) & (row < rows_here)
    vm[0:sets, :] = frame * pix_count + row * W + (idx_ref[...] & 511)
    bit = lax.broadcasted_iota(jnp.int32, owned.shape, 0)
    word = jnp.sum(jnp.where(owned, jnp.left_shift(1, bit), 0), axis=0, keepdims=True)
    word = word | jnp.left_shift(pltpu.roll(word, groups // 2, axis=1), sets)
    vm[sets : sets + 8, :] = jnp.broadcast_to(word, (8, groups))
    to_scalar = pltpu.make_async_copy(vm, sm, sems)
    to_scalar.start()
    to_scalar.wait()

    def copy(k, pix):
        first = pl.multiple_of(pix & ~15, 16)
        return pltpu.make_async_copy(
            feat_ref.at[pl.ds(first, 16), :], slots.at[pl.ds(pl.multiple_of(k * 16, 16), 16), :], sem
        )

    def group(g, count):
        def step(state):
            left, count = state
            i = 31 - lax.clz(left & -left)
            at, lane = i & (sets - 1), g + lax.shift_right_logical(i, sets.bit_length() - 1) * (groups // 2)
            pix = sm[at, lane]
            copy(count, pix).start()
            found_at[0, count] = at * groups + lane
            found_at[1, count] = pix & 15
            return left & (left - 1), count + 1

        return lax.while_loop(lambda state: state[0] != 0, step, (sm[sets, g], count))[1]

    found = lax.fori_loop(0, groups // 2, group, 0)
    for k in range(BATCH - 1):
        found_at[0, found + k] = lines.shape[0] - 8
        found_at[1, found + k] = 0

    def wait(rows):
        def step(k, carry):
            pltpu.make_async_copy(feat_ref.at[pl.ds(0, rows), :], slots.at[pl.ds(0, rows), :], sem).wait()
            return carry

        return step

    lax.fori_loop(0, lax.shift_right_logical(found, 3), wait(128), 0)
    lax.fori_loop(0, found & 7, wait(16), 0)

    def place(batch, carry):
        for k in range(BATCH):
            at = pl.multiple_of((batch * BATCH + k) * 16, 16)
            wide[k] = slots[pl.ds(at, 16), :].astype(jnp.float32)
        picked = [wide[k, pl.ds(found_at[1, batch * BATCH + k], 1), :] for k in range(BATCH)]
        for k in range(BATCH):
            lines[pl.ds(found_at[0, batch * BATCH + k], 1), :] = picked[k]
        return carry

    lax.fori_loop(0, lax.div(found + BATCH - 1, BATCH), place, 0)
    mine = pl.multiple_of(core * half, half)
    theirs = pl.multiple_of((1 - core) * half, half)
    keep_ref[...] = (lines[pl.ds(mine, half), :] * 0.0625).astype(keep_ref.dtype)
    send_ref[...] = (lines[pl.ds(theirs, half), :] * 0.0625).astype(send_ref.dtype)


def pick(features, query_frame, query_row, query_col, rows_here):
    flat = features.reshape(-1, features.shape[2])
    queries, chan = query_frame.shape[0], features.shape[2]
    lanes = 128
    sets = queries // lanes
    half = jax.ShapeDtypeStruct((queries // 2, chan), features.dtype)
    vmem = pl.BlockSpec(memory_space=pltpu.VMEM)
    hbm = pl.BlockSpec(memory_space=pltpu.MemorySpace.HBM)
    return pl.pallas_call(
        functools.partial(pick_kernel, rows_here),
        out_shape=(half, half),
        in_specs=[vmem, hbm],
        out_specs=(vmem, vmem),
        scratch_shapes=[
            pltpu.VMEM((sets + 8, lanes), jnp.int32),
            pltpu.SMEM((sets + 8, lanes), jnp.int32),
            pltpu.SMEM((2, queries + BATCH), jnp.int32),
            pltpu.VMEM(((queries + BATCH) * 16, chan), features.dtype),
            pltpu.VMEM((BATCH, 16, chan), jnp.float32),
            pltpu.VMEM((queries + 8, chan), jnp.float32),
            pltpu.SemaphoreType.DMA,
            pltpu.SemaphoreType.DMA,
        ],
        compiler_params=pltpu.CompilerParams(vmem_limit_bytes=51 << 20),
        name="pick",
    )((query_frame * 2**18 + query_row * 2**9 + query_col).reshape(sets, lanes), flat)


BLOCK = 256
PARTS = 5
UNITS = 2


def score_kernel(own_ref, other_ref, first_ref, feat_ref, out_ref, rest, even, odd, sem):
    tile_idx = lax.axis_index("tile")
    core = tile_idx % 2
    load = pltpu.make_async_copy(feat_ref.at[pl.ds(1, rest.shape[0])], rest, sem)
    load.start()
    frames, rows_here = 1 + rest.shape[0], rest.shape[1]
    cols = W // PARTS
    half_blocks = own_ref.shape[0] // BLOCK
    blocks = 2 * half_blocks
    pairs = blocks // UNITS
    steps = frames * pairs
    total_rows = float(rows_here * lax.axis_size("tile"))
    first_row = (tile_idx * rows_here).astype(jnp.float32)
    sub = lax.broadcasted_iota(jnp.int32, (8, BLOCK), 0).astype(jnp.float32)
    zero = jnp.zeros((8, BLOCK), jnp.float32)
    low = jnp.full((8, BLOCK), -jnp.inf, jnp.float32)

    def stage(pair):
        for m in range(UNITS):
            ref, k = (own_ref, pair * UNITS + m) if pair * UNITS < half_blocks else (other_ref, pair * UNITS + m - half_blocks)
            pltpu.matmul_push_rhs(ref[k * BLOCK : (k + 1) * BLOCK, :], 0, m, transpose=True)

    def run(*accs):
        def moves(f, part, staged, kept, was, tops):
            for r in range(rows_here):
                seen = None if tops is None else []
                if tops is not None:
                    for m in range(UNITS):
                        scores = pltpu.matmul_pop(accs[m * rows_here + r])
                        kept[was, m, r * cols : (r + 1) * cols, :] = scores
                        tops[m] = jnp.maximum(tops[m], jnp.max(scores.reshape(cols // 8, 8, BLOCK), axis=0))
                        seen.append(scores[cols - 8 : cols, :])
                if f is not None:
                    at = pl.ds(pl.multiple_of(part * cols, 16), cols)
                    lhs = first_ref[r, at, :] if f == 0 else rest[f - 1, r, at, :]
                    for m in range(UNITS):
                        pltpu.matmul_acc_lhs(accs[m * rows_here + r], lhs, load_staged_rhs=staged if r == 0 else None)
                yield seen

        def weighs(kept, part, peaks, sums):
            start = jnp.asarray(part * cols).astype(jnp.float32)
            here, across = [None] * UNITS, [None] * UNITS
            for k in reversed(range(cols // 8)):
                for m in range(UNITS):
                    tail, below = None, None
                    for r in reversed(range(rows_here)):
                        at = r * cols + k * 8
                        expo = jnp.exp2((kept[part, m, at : at + 8, :] - peaks[m]) * LOG2E)
                        tail = expo if tail is None else tail + expo
                        if r > 0:
                            below = tail if below is None else below + tail
                    sums[m][2] = sums[m][2] + below
                    here[m] = tail if here[m] is None else here[m] + tail
                    if k > 0:
                        across[m] = here[m] if across[m] is None else across[m] + here[m]
                    yield
            for m in range(UNITS):
                sums[m][0] = sums[m][0] + here[m]
                sums[m][1] = sums[m][1] + (across[m] * 8.0 + here[m] * (sub + start))

        def weave(moving, weighing, peaks):
            per = (cols // 8) * UNITS // rows_here
            if moving is None:
                moving = iter(())
            if weighing is None:
                weighing = iter(())
            for turn in range(rows_here):
                seen = next(moving, None)
                if seen is not None and peaks is not None and turn % 4 == 0:
                    for m in range(UNITS):
                        peaks[m] = jnp.minimum(peaks[m], jnp.maximum(peaks[m], seen[m]))
                for _ in range(per):
                    next(weighing, None)
            for _ in moving:
                pass
            for _ in weighing:
                pass

        def settle(tops):
            return tuple(jnp.broadcast_to(jnp.max(t, axis=0, keepdims=True), t.shape) for t in tops)

        def finish(step, peaks, sums):
            f, pair = divmod(step, pairs)
            for m in range(UNITS):
                total, sum_x, sum_y = [jnp.sum(a, axis=0, keepdims=True) for a in sums[m]]
                where_to = lax.rem(pair * UNITS + m + core * half_blocks, blocks)
                packed = jnp.concatenate(
                    [peaks[m][0:1], total, sum_x * (1.0 / W), (sum_y + first_row * total) * (1.0 / total_rows)], axis=0
                )
                for side in range(2):
                    out_ref[side, where_to, f] = packed

        none, fresh = (low,) * UNITS, ((zero, zero, zero),) * UNITS
        stage(0)
        tops, peaks, sums = None, None, None
        for step in range(steps + 2):
            f = step // pairs if step < steps else None
            new, old = (even, odd) if step % 2 == 0 else (odd, even)
            if step == pairs:
                load.wait()
            last_peaks = peaks
            tops = None if tops is None else list(tops)
            sums = None if sums is None else [list(x) for x in sums]
            bound = None if last_peaks is None else list(last_peaks)
            weave(
                moves(f, 0, 0, old, PARTS - 1, tops) if step <= steps else None,
                weighs(new, PARTS - 1, bound, sums) if step > 1 else None,
                bound,
            )
            if step <= steps:
                peaks = None if tops is None else settle(tops)
            if step + 1 < steps:
                stage((step + 1) % pairs)
            if step > 1:
                finish(step - 2, last_peaks, sums)
            if step > steps:
                break

            def part_of(i, state):
                tops, sums = state
                tops, sums = list(tops), [list(x) for x in sums]
                bound = None if peaks is None else list(peaks)
                weave(
                    moves(f, i, None, new, i - 1, tops) if step < steps else None,
                    weighs(old, i - 1, bound, sums) if step > 0 else None,
                    bound,
                )
                tops, sums = tuple(tops), tuple(tuple(x) for x in sums)
                return tops, sums

            tops, sums = lax.fori_loop(1, PARTS, part_of, (none, fresh))

    pl.run_scoped(
        run, *[pltpu.ACC(m)((cols, BLOCK), jnp.float32) for m in range(UNITS) for _ in range(rows_here)]
    )


def fetch_kernel(feat_ref, own_ref, out_ref, sem):
    load = pltpu.make_async_copy(feat_ref.at[0], out_ref, sem)
    load.start()
    load.wait()


def fetch(features, own):
    hbm = pl.BlockSpec(memory_space=pltpu.MemorySpace.HBM)
    return pl.pallas_call(
        fetch_kernel,
        out_shape=jax.ShapeDtypeStruct(features.shape[1:], features.dtype),
        in_specs=[hbm, pl.BlockSpec(memory_space=pl.ANY)],
        out_specs=pl.BlockSpec(memory_space=pltpu.VMEM),
        scratch_shapes=[pltpu.SemaphoreType.DMA],
        compiler_params=pltpu.CompilerParams(vmem_limit_bytes=49 << 20),
        cost_estimate=pl.CostEstimate(flops=0, bytes_accessed=4 << 20, transcendentals=0),
        name="fetch",
    )(features, own)


def score(own, other, first, features, rows_here):
    frames, pix_count, chan = features.shape
    blocks = 2 * own.shape[0] // BLOCK
    vmem = pl.BlockSpec(memory_space=pltpu.VMEM)
    kept = pltpu.VMEM((PARTS, UNITS, pix_count // PARTS, BLOCK), jnp.float32)
    return pl.pallas_call(
        score_kernel,
        out_shape=jax.ShapeDtypeStruct((2, blocks, frames, 4, BLOCK), jnp.float32),
        in_specs=[vmem, vmem, vmem, pl.BlockSpec(memory_space=pltpu.MemorySpace.HBM)],
        out_specs=vmem,
        scratch_shapes=[
            pltpu.VMEM((frames - 1, rows_here, W, chan), features.dtype),
            kept,
            kept,
            pltpu.SemaphoreType.DMA,
        ],
        compiler_params=pltpu.CompilerParams(vmem_limit_bytes=49 << 20),
        name="score",
    )(own, other, first.reshape(rows_here, W, chan), features.reshape(frames, rows_here, W, chan))


def merge_kernel(pixels, parts_ref, inputs_ref, far_ref, near_ref):
    tiles, frames = parts_ref.shape[1], parts_ref.shape[2]
    frame_idx = lax.axis_index("frame")
    here, y = frame_idx // 4 % 2, frame_idx % 4
    odd = y % 2

    def joined(side, f):
        parts = [parts_ref[side, k, f] for k in range(tiles)]
        peak = functools.reduce(jnp.maximum, [p[0:1] for p in parts])
        sums = functools.reduce(jnp.add, [p[1:4] * jnp.exp(p[0:1] - peak) for p in parts])
        total = sums[0:1]
        log_total = jnp.log(total)
        return jnp.concatenate(
            [sums[1:2] / total, sums[2:3] / total, -log_total, peak + log_total - math.log(pixels)], axis=0
        )

    for f in range(frames):
        inputs_ref[f] = joined(here, f)
    across = joined(1 - here, odd * (frames - 1))
    first, last = inputs_ref[0], inputs_ref[frames - 1]
    far_ref[...] = jnp.where((y == 0) | (y == 3), across, jnp.where(odd == 1, last, first))
    near_ref[...] = jnp.where(odd == 1, first, last)


def merge(parts, pixels):
    _, _, frames, stats, share = parts.shape
    vmem = pl.BlockSpec(memory_space=pltpu.VMEM)
    edge = jax.ShapeDtypeStruct((stats, share), jnp.float32)
    return pl.pallas_call(
        functools.partial(merge_kernel, pixels),
        out_shape=(jax.ShapeDtypeStruct((frames, stats, share), jnp.float32), edge, edge),
        in_specs=[vmem],
        out_specs=(vmem, vmem, vmem),
        compiler_params=pltpu.CompilerParams(vmem_limit_bytes=4 << 20),
        name="merge",
    )(parts)


def split(array, count):
    parts = []
    for _ in range(count):
        parts.append(array.astype(jnp.bfloat16))
        array = array - parts[-1].astype(jnp.float32)
    return parts


MEET = ((0, 0), (0, 1), (1, 0), (1, 1), (0, 2), (2, 0))
DEPTH = 128


def prepare_kernel(weight_ref, bias_ref, out_weight_ref, taps_ref, last_ref):
    taps, stats, hidden = weight_ref.shape
    rows = jnp.concatenate([weight_ref[k] for k in range(taps)] + [jnp.broadcast_to(bias_ref[...], (4, hidden))], axis=0)
    thirds = [p.astype(jnp.float32) for p in split(rows, 3)]
    stacked = jnp.concatenate([thirds[i] for i, _ in MEET], axis=0)
    filler = jnp.zeros((DEPTH - stacked.shape[0], hidden), jnp.float32)
    taps_ref[...] = jnp.transpose(jnp.concatenate([stacked, filler], axis=0)).astype(jnp.bfloat16)
    thirds = [p.astype(jnp.float32) for p in split(out_weight_ref[...], 2)]
    filler = jnp.zeros((8 - out_weight_ref.shape[0], hidden), jnp.float32)
    last_ref[...] = jnp.concatenate([thirds[0], filler, thirds[1], filler], axis=0).astype(jnp.bfloat16)


def prepare(conv_weight, conv_bias, out_weight):
    hidden = conv_bias.shape[0]
    vmem = pl.BlockSpec(memory_space=pltpu.VMEM)
    return pl.pallas_call(
        prepare_kernel,
        out_shape=(
            jax.ShapeDtypeStruct((hidden, DEPTH), jnp.bfloat16),
            jax.ShapeDtypeStruct((16, hidden), jnp.bfloat16),
        ),
        in_specs=[vmem] * 3,
        out_specs=(vmem, vmem),
        cost_estimate=pl.CostEstimate(flops=200000, bytes_accessed=200000, transcendentals=0),
        compiler_params=pltpu.CompilerParams(vmem_limit_bytes=8 << 20),
        name="prepare",
    )(conv_weight, conv_bias[None, :], out_weight)


def refine_kernel(far_ref, inputs_ref, near_ref, taps_ref, last_ref, out_ref, held, sem):
    frames, share = inputs_ref.shape[0], inputs_ref.shape[2]
    odd = lax.axis_index("frame") % 2 == 1
    far, near = far_ref[...], near_ref[...]
    before, after = jnp.where(odd, near, far), jnp.where(odd, far, near)
    line = [before] + [inputs_ref[f] for f in range(frames)] + [after]
    unit = jnp.where(lax.broadcasted_iota(jnp.int32, (4, share), 0) == 0, 1.0, 0.0)
    right = []
    for f in range(frames):
        rows = jnp.concatenate([line[f + k] for k in range(3)] + [unit], axis=0)
        thirds = [p.astype(jnp.float32) for p in split(rows, 3)]
        stacked = jnp.concatenate([thirds[j] for _, j in MEET], axis=0)
        filler = jnp.zeros((DEPTH - stacked.shape[0], share), jnp.float32)
        right.append(jnp.concatenate([stacked, filler], axis=0).astype(jnp.bfloat16))
    for f in range(frames):
        acc = jnp.dot(taps_ref[...], right[f], preferred_element_type=jnp.float32)
        hidden = jax.nn.gelu(acc)
        high, rest = split(hidden, 2)
        first = jnp.dot(last_ref[...], high, preferred_element_type=jnp.float32)
        second = jnp.dot(last_ref[...], rest, preferred_element_type=jnp.float32)
        delta = first[0:3] + (first[8:11] + second[0:3])
        moved = line[f + 1][0:3] + delta
        for o in range(3):
            held[o, f : f + 1] = moved[o : o + 1]
    store = pltpu.make_async_copy(held, out_ref, sem)
    store.start()
    store.wait()


def refine(far, inputs, near, taps, last):
    frames, _, share = inputs.shape
    moved = pl.pallas_call(
        refine_kernel,
        out_shape=jax.ShapeDtypeStruct((3, frames, share), jnp.float32),
        in_specs=[pl.BlockSpec(memory_space=pltpu.VMEM)] * 5,
        out_specs=pl.BlockSpec(memory_space=pltpu.MemorySpace.HBM),
        scratch_shapes=[pltpu.VMEM((3, frames, share), jnp.float32), pltpu.SemaphoreType.DMA],
        compiler_params=pltpu.CompilerParams(vmem_limit_bytes=8 << 20),
        name="refine",
    )(far, inputs, near, taps, last)
    return jnp.transpose(moved, (1, 0, 2))


def local(features, query_frame, query_row, query_col, conv_weight, conv_bias, out_weight):
    frame_count, pix_count, chan = features.shape
    rows_here = pix_count // W
    tiles, groups = lax.axis_size("tile"), lax.axis_size("frame")
    plane, column, tower = mesh_groups()
    keep, send = pick(features, query_frame, query_row, query_col, rows_here)
    swap = [(i, i ^ 1) for i in range(tiles)]
    mine = keep + lax.ppermute(send, "tile", swap)
    wide, tall = len(plane[0]), len(column[0])
    rows = mine.shape[0] // wide
    got = lax.all_to_all(mine.reshape(wide, rows, chan), "frame", 0, 0, axis_index_groups=plane)
    piece = jnp.sum(got, axis=0)
    got = lax.all_to_all(jnp.broadcast_to(piece, (tall, rows, chan)), BOTH, 0, 0, axis_index_groups=column)
    piece = jnp.sum(got, axis=0)
    got = lax.all_to_all(jnp.broadcast_to(piece, (wide, rows, chan)), "frame", 0, 0, axis_index_groups=plane)
    own = got.reshape(wide * rows, chan)
    other = lax.ppermute(own, "tile", swap)
    parts = score(own, other, fetch(features, own), features, rows_here)
    members = 2 * tiles
    shape = parts.shape
    parts = lax.all_to_all(parts.reshape(members, *shape[2:]), BOTH, 0, 0, axis_index_groups=tower)
    inputs, far, near = merge(parts.reshape(shape), rows_here * tiles * W)
    far = lax.ppermute(far, "frame", far_pairs())
    near = lax.ppermute(near, "frame", [(i, i ^ 1) for i in range(groups)])
    taps, last_weight = prepare(conv_weight, conv_bias, out_weight)
    return refine(far, inputs, near, taps, last_weight)


def solution(mesh):
    in_specs = (P("frame", "tile", None), P(), P(), P(), P(), P(), P())
    out_specs = P("frame", None, "tile")
    return jax.shard_map(local, mesh=mesh, in_specs=in_specs, out_specs=out_specs, check_vma=False)
```

```python
import functools
import math

import jax
import jax.numpy as jnp
from jax import lax
from jax.experimental import pallas as pl
from jax.experimental.pallas import tpu as pltpu
from jax.sharding import PartitionSpec as P

W = 480
LOG2E = math.log2(math.e)
BOTH = ("frame", "tile")


def mesh_groups():
    plane = [[x * 8 + zh * 4 + y for x in range(4) for y in range(4)] for zh in range(2)]
    column = [
        [(x * 8 + zh * 4 + y) * 8 + zl * 2 + c for zh in range(2) for zl in range(4)]
        for x in range(4)
        for y in range(4)
        for c in range(2)
    ]
    tower = [[(x * 8 + zh * 4 + y) * 8 + t for zh in range(2) for t in range(8)] for x in range(4) for y in range(4)]
    return plane, column, tower


def far_pairs():
    pairs = []
    for i in range(32):
        x, zh, y = i // 8, i // 4 % 2, i % 4
        if y in (1, 2):
            pairs.append((i, i + 1 if y == 1 else i - 1))
        elif y == 3 and (zh == 1 or x < 3):
            pairs.append((i, (x + 1 - zh) * 8 + zh * 4))
        elif y == 0 and (zh == 0 or x > 0):
            pairs.append((i, (x - zh) * 8 + zh * 4 + 3))
    return pairs


BATCH = 4


def pick_kernel(rows_here, idx_ref, feat_ref, keep_ref, send_ref, vm, sm, found_at, slots, wide, lines, sems, sem):
    frame_idx, tile_idx = lax.axis_index("frame"), lax.axis_index("tile")
    core = tile_idx % 2
    pix_count = rows_here * W
    frame_count = feat_ref.shape[0] // pix_count
    half = keep_ref.shape[0]
    sets, groups = idx_ref.shape
    lines[...] = jnp.zeros_like(lines)
    frame = jnp.right_shift(idx_ref[...], 18) - frame_idx * frame_count
    row = (jnp.right_shift(idx_ref[...], 9) & 511) - tile_idx * rows_here
    owned = (frame >= 0) & (frame < frame_count) & (row >= 0) & (row < rows_here)
    vm[0:sets, :] = frame * pix_count + row * W + (idx_ref[...] & 511)
    bit = lax.broadcasted_iota(jnp.int32, owned.shape, 0)
    word = jnp.sum(jnp.where(owned, jnp.left_shift(1, bit), 0), axis=0, keepdims=True)
    word = word | jnp.left_shift(pltpu.roll(word, groups // 2, axis=1), sets)
    vm[sets : sets + 8, :] = jnp.broadcast_to(word, (8, groups))
    to_scalar = pltpu.make_async_copy(vm, sm, sems)
    to_scalar.start()
    to_scalar.wait()

    def copy(k, pix):
        first = pl.multiple_of(pix & ~15, 16)
        return pltpu.make_async_copy(
            feat_ref.at[pl.ds(first, 16), :], slots.at[pl.ds(pl.multiple_of(k * 16, 16), 16), :], sem
        )

    def group(g, count):
        def step(state):
            left, count = state
            i = 31 - lax.clz(left & -left)
            at, lane = i & (sets - 1), g + lax.shift_right_logical(i, sets.bit_length() - 1) * (groups // 2)
            pix = sm[at, lane]
            copy(count, pix).start()
            found_at[0, count] = at * groups + lane
            found_at[1, count] = pix & 15
            return left & (left - 1), count + 1

        return lax.while_loop(lambda state: state[0] != 0, step, (sm[sets, g], count))[1]

    found = lax.fori_loop(0, groups // 2, group, 0)
    for k in range(BATCH - 1):
        found_at[0, found + k] = lines.shape[0] - 8
        found_at[1, found + k] = 0

    def wait(rows):
        def step(k, carry):
            pltpu.make_async_copy(feat_ref.at[pl.ds(0, rows), :], slots.at[pl.ds(0, rows), :], sem).wait()
            return carry

        return step

    lax.fori_loop(0, lax.shift_right_logical(found, 3), wait(128), 0)
    lax.fori_loop(0, found & 7, wait(16), 0)

    def place(batch, carry):
        for k in range(BATCH):
            at = pl.multiple_of((batch * BATCH + k) * 16, 16)
            wide[k] = slots[pl.ds(at, 16), :].astype(jnp.float32)
        picked = [wide[k, pl.ds(found_at[1, batch * BATCH + k], 1), :] for k in range(BATCH)]
        for k in range(BATCH):
            lines[pl.ds(found_at[0, batch * BATCH + k], 1), :] = picked[k]
        return carry

    lax.fori_loop(0, lax.div(found + BATCH - 1, BATCH), place, 0)
    mine = pl.multiple_of(core * half, half)
    theirs = pl.multiple_of((1 - core) * half, half)
    keep_ref[...] = (lines[pl.ds(mine, half), :] * 0.0625).astype(keep_ref.dtype)
    send_ref[...] = (lines[pl.ds(theirs, half), :] * 0.0625).astype(send_ref.dtype)


def pick(features, query_frame, query_row, query_col, rows_here):
    flat = features.reshape(-1, features.shape[2])
    queries, chan = query_frame.shape[0], features.shape[2]
    lanes = 128
    sets = queries // lanes
    half = jax.ShapeDtypeStruct((queries // 2, chan), features.dtype)
    vmem = pl.BlockSpec(memory_space=pltpu.VMEM)
    hbm = pl.BlockSpec(memory_space=pltpu.MemorySpace.HBM)
    return pl.pallas_call(
        functools.partial(pick_kernel, rows_here),
        out_shape=(half, half),
        in_specs=[vmem, hbm],
        out_specs=(vmem, vmem),
        scratch_shapes=[
            pltpu.VMEM((sets + 8, lanes), jnp.int32),
            pltpu.SMEM((sets + 8, lanes), jnp.int32),
            pltpu.SMEM((2, queries + BATCH), jnp.int32),
            pltpu.VMEM(((queries + BATCH) * 16, chan), features.dtype),
            pltpu.VMEM((BATCH, 16, chan), jnp.float32),
            pltpu.VMEM((queries + 8, chan), jnp.float32),
            pltpu.SemaphoreType.DMA,
            pltpu.SemaphoreType.DMA,
        ],
        compiler_params=pltpu.CompilerParams(vmem_limit_bytes=51 << 20),
        name="pick",
    )((query_frame * 2**18 + query_row * 2**9 + query_col).reshape(sets, lanes), flat)


BLOCK = 256
PARTS = 5
UNITS = 2


def score_kernel(own_ref, other_ref, first_ref, feat_ref, out_ref, rest, even, odd, sem):
    tile_idx = lax.axis_index("tile")
    core = tile_idx % 2
    load = pltpu.make_async_copy(feat_ref.at[pl.ds(1, rest.shape[0])], rest, sem)
    load.start()
    frames, rows_here = 1 + rest.shape[0], rest.shape[1]
    cols = W // PARTS
    half_blocks = own_ref.shape[0] // BLOCK
    blocks = 2 * half_blocks
    pairs = blocks // UNITS
    steps = frames * pairs
    total_rows = float(rows_here * lax.axis_size("tile"))
    first_row = (tile_idx * rows_here).astype(jnp.float32)
    sub = lax.broadcasted_iota(jnp.int32, (8, BLOCK), 0).astype(jnp.float32)
    zero = jnp.zeros((8, BLOCK), jnp.float32)
    low = jnp.full((8, BLOCK), -jnp.inf, jnp.float32)

    def stage(pair):
        for m in range(UNITS):
            ref, k = (own_ref, pair * UNITS + m) if pair * UNITS < half_blocks else (other_ref, pair * UNITS + m - half_blocks)
            pltpu.matmul_push_rhs(ref[k * BLOCK : (k + 1) * BLOCK, :], 0, m, transpose=True)

    def run(*accs):
        def moves(f, part, staged, kept, was, tops):
            for r in range(rows_here):
                seen = None if tops is None else []
                if tops is not None:
                    for m in range(UNITS):
                        scores = pltpu.matmul_pop(accs[m * rows_here + r])
                        kept[was, m, r * cols : (r + 1) * cols, :] = scores
                        tops[m] = jnp.maximum(tops[m], jnp.max(scores.reshape(cols // 8, 8, BLOCK), axis=0))
                        seen.append(scores[cols - 8 : cols, :])
                if f is not None:
                    at = pl.ds(pl.multiple_of(part * cols, 16), cols)
                    lhs = first_ref[r, at, :] if f == 0 else rest[f - 1, r, at, :]
                    for m in range(UNITS):
                        pltpu.matmul_acc_lhs(accs[m * rows_here + r], lhs, load_staged_rhs=staged if r == 0 else None)
                yield seen

        def weighs(kept, part, peaks, sums):
            start = jnp.asarray(part * cols).astype(jnp.float32)
            here, across = [None] * UNITS, [None] * UNITS
            for k in reversed(range(cols // 8)):
                for m in range(UNITS):
                    tail, below = None, None
                    for r in reversed(range(rows_here)):
                        at = r * cols + k * 8
                        expo = jnp.exp2((kept[part, m, at : at + 8, :] - peaks[m]) * LOG2E)
                        tail = expo if tail is None else tail + expo
                        if r > 0:
                            below = tail if below is None else below + tail
                    sums[m][2] = sums[m][2] + below
                    here[m] = tail if here[m] is None else here[m] + tail
                    if k > 0:
                        across[m] = here[m] if across[m] is None else across[m] + here[m]
                    yield
            for m in range(UNITS):
                sums[m][0] = sums[m][0] + here[m]
                sums[m][1] = sums[m][1] + (across[m] * 8.0 + here[m] * (sub + start))

        def weave(moving, weighing, peaks):
            per = (cols // 8) * UNITS // rows_here
            if moving is None:
                moving = iter(())
            if weighing is None:
                weighing = iter(())
            for turn in range(rows_here):
                seen = next(moving, None)
                if seen is not None and peaks is not None and turn % 4 == 0:
                    for m in range(UNITS):
                        peaks[m] = jnp.minimum(peaks[m], jnp.maximum(peaks[m], seen[m]))
                for _ in range(per):
                    next(weighing, None)
            for _ in moving:
                pass
            for _ in weighing:
                pass

        def settle(tops):
            return tuple(jnp.broadcast_to(jnp.max(t, axis=0, keepdims=True), t.shape) for t in tops)

        def finish(step, peaks, sums):
            f, pair = divmod(step, pairs)
            for m in range(UNITS):
                total, sum_x, sum_y = [jnp.sum(a, axis=0, keepdims=True) for a in sums[m]]
                where_to = lax.rem(pair * UNITS + m + core * half_blocks, blocks)
                packed = jnp.concatenate(
                    [peaks[m][0:1], total, sum_x * (1.0 / W), (sum_y + first_row * total) * (1.0 / total_rows)], axis=0
                )
                for side in range(2):
                    out_ref[side, where_to, f] = packed

        none, fresh = (low,) * UNITS, ((zero, zero, zero),) * UNITS
        stage(0)
        tops, peaks, sums = None, None, None
        for step in range(steps + 2):
            f = step // pairs if step < steps else None
            new, old = (even, odd) if step % 2 == 0 else (odd, even)
            if step == pairs:
                load.wait()
            last_peaks = peaks
            tops = None if tops is None else list(tops)
            sums = None if sums is None else [list(x) for x in sums]
            bound = None if last_peaks is None else list(last_peaks)
            weave(
                moves(f, 0, 0, old, PARTS - 1, tops) if step <= steps else None,
                weighs(new, PARTS - 1, bound, sums) if step > 1 else None,
                bound,
            )
            if step <= steps:
                peaks = None if tops is None else settle(tops)
            if step + 1 < steps:
                stage((step + 1) % pairs)
            if step > 1:
                finish(step - 2, last_peaks, sums)
            if step > steps:
                break

            def part_of(i, state):
                tops, sums = state
                tops, sums = list(tops), [list(x) for x in sums]
                bound = None if peaks is None else list(peaks)
                weave(
                    moves(f, i, None, new, i - 1, tops) if step < steps else None,
                    weighs(old, i - 1, bound, sums) if step > 0 else None,
                    bound,
                )
                tops, sums = tuple(tops), tuple(tuple(x) for x in sums)
                return tops, sums

            tops, sums = lax.fori_loop(1, PARTS, part_of, (none, fresh))

    pl.run_scoped(
        run, *[pltpu.ACC(m)((cols, BLOCK), jnp.float32) for m in range(UNITS) for _ in range(rows_here)]
    )


def fetch_kernel(feat_ref, own_ref, out_ref, sem):
    load = pltpu.make_async_copy(feat_ref.at[0], out_ref, sem)
    load.start()
    load.wait()


def fetch(features, own):
    hbm = pl.BlockSpec(memory_space=pltpu.MemorySpace.HBM)
    return pl.pallas_call(
        fetch_kernel,
        out_shape=jax.ShapeDtypeStruct(features.shape[1:], features.dtype),
        in_specs=[hbm, pl.BlockSpec(memory_space=pl.ANY)],
        out_specs=pl.BlockSpec(memory_space=pltpu.VMEM),
        scratch_shapes=[pltpu.SemaphoreType.DMA],
        compiler_params=pltpu.CompilerParams(vmem_limit_bytes=49 << 20),
        cost_estimate=pl.CostEstimate(flops=0, bytes_accessed=4 << 20, transcendentals=0),
        name="fetch",
    )(features, own)


def score(own, other, first, features, rows_here):
    frames, pix_count, chan = features.shape
    blocks = 2 * own.shape[0] // BLOCK
    vmem = pl.BlockSpec(memory_space=pltpu.VMEM)
    kept = pltpu.VMEM((PARTS, UNITS, pix_count // PARTS, BLOCK), jnp.float32)
    return pl.pallas_call(
        score_kernel,
        out_shape=jax.ShapeDtypeStruct((2, blocks, frames, 4, BLOCK), jnp.float32),
        in_specs=[vmem, vmem, vmem, pl.BlockSpec(memory_space=pltpu.MemorySpace.HBM)],
        out_specs=vmem,
        scratch_shapes=[
            pltpu.VMEM((frames - 1, rows_here, W, chan), features.dtype),
            kept,
            kept,
            pltpu.SemaphoreType.DMA,
        ],
        compiler_params=pltpu.CompilerParams(vmem_limit_bytes=49 << 20),
        name="score",
    )(own, other, first.reshape(rows_here, W, chan), features.reshape(frames, rows_here, W, chan))


def merge_kernel(pixels, parts_ref, inputs_ref, far_ref, near_ref):
    tiles, frames = parts_ref.shape[1], parts_ref.shape[2]
    frame_idx = lax.axis_index("frame")
    here, y = frame_idx // 4 % 2, frame_idx % 4
    odd = y % 2

    def joined(side, f):
        parts = [parts_ref[side, k, f] for k in range(tiles)]
        peak = functools.reduce(jnp.maximum, [p[0:1] for p in parts])
        sums = functools.reduce(jnp.add, [p[1:4] * jnp.exp(p[0:1] - peak) for p in parts])
        total = sums[0:1]
        log_total = jnp.log(total)
        return jnp.concatenate(
            [sums[1:2] / total, sums[2:3] / total, -log_total, peak + log_total - math.log(pixels)], axis=0
        )

    for f in range(frames):
        inputs_ref[f] = joined(here, f)
    across = joined(1 - here, odd * (frames - 1))
    first, last = inputs_ref[0], inputs_ref[frames - 1]
    far_ref[...] = jnp.where((y == 0) | (y == 3), across, jnp.where(odd == 1, last, first))
    near_ref[...] = jnp.where(odd == 1, first, last)


def merge(parts, pixels):
    _, _, frames, stats, share = parts.shape
    vmem = pl.BlockSpec(memory_space=pltpu.VMEM)
    edge = jax.ShapeDtypeStruct((stats, share), jnp.float32)
    return pl.pallas_call(
        functools.partial(merge_kernel, pixels),
        out_shape=(jax.ShapeDtypeStruct((frames, stats, share), jnp.float32), edge, edge),
        in_specs=[vmem],
        out_specs=(vmem, vmem, vmem),
        compiler_params=pltpu.CompilerParams(vmem_limit_bytes=4 << 20),
        name="merge",
    )(parts)


def split(array, count):
    parts = []
    for _ in range(count):
        parts.append(array.astype(jnp.bfloat16))
        array = array - parts[-1].astype(jnp.float32)
    return parts


MEET = ((0, 0), (0, 1), (1, 0), (1, 1), (0, 2), (2, 0))
DEPTH = 128


def prepare_kernel(weight_ref, bias_ref, out_weight_ref, taps_ref, last_ref):
    taps, stats, hidden = weight_ref.shape
    rows = jnp.concatenate([weight_ref[k] for k in range(taps)] + [jnp.broadcast_to(bias_ref[...], (4, hidden))], axis=0)
    thirds = [p.astype(jnp.float32) for p in split(rows, 3)]
    stacked = jnp.concatenate([thirds[i] for i, _ in MEET], axis=0)
    filler = jnp.zeros((DEPTH - stacked.shape[0], hidden), jnp.float32)
    taps_ref[...] = jnp.transpose(jnp.concatenate([stacked, filler], axis=0)).astype(jnp.bfloat16)
    thirds = [p.astype(jnp.float32) for p in split(out_weight_ref[...], 2)]
    filler = jnp.zeros((8 - out_weight_ref.shape[0], hidden), jnp.float32)
    last_ref[...] = jnp.concatenate([thirds[0], filler, thirds[1], filler], axis=0).astype(jnp.bfloat16)


def prepare(conv_weight, conv_bias, out_weight):
    hidden = conv_bias.shape[0]
    vmem = pl.BlockSpec(memory_space=pltpu.VMEM)
    return pl.pallas_call(
        prepare_kernel,
        out_shape=(
            jax.ShapeDtypeStruct((hidden, DEPTH), jnp.bfloat16),
            jax.ShapeDtypeStruct((16, hidden), jnp.bfloat16),
        ),
        in_specs=[vmem] * 3,
        out_specs=(vmem, vmem),
        cost_estimate=pl.CostEstimate(flops=200000, bytes_accessed=200000, transcendentals=0),
        compiler_params=pltpu.CompilerParams(vmem_limit_bytes=8 << 20),
        name="prepare",
    )(conv_weight, conv_bias[None, :], out_weight)


def refine_kernel(far_ref, inputs_ref, near_ref, taps_ref, last_ref, out_ref, held, sem):
    frames, share = inputs_ref.shape[0], inputs_ref.shape[2]
    odd = lax.axis_index("frame") % 2 == 1
    far, near = far_ref[...], near_ref[...]
    before, after = jnp.where(odd, near, far), jnp.where(odd, far, near)
    line = [before] + [inputs_ref[f] for f in range(frames)] + [after]
    unit = jnp.where(lax.broadcasted_iota(jnp.int32, (4, share), 0) == 0, 1.0, 0.0)
    right = []
    for f in range(frames):
        rows = jnp.concatenate([line[f + k] for k in range(3)] + [unit], axis=0)
        thirds = [p.astype(jnp.float32) for p in split(rows, 3)]
        stacked = jnp.concatenate([thirds[j] for _, j in MEET], axis=0)
        filler = jnp.zeros((DEPTH - stacked.shape[0], share), jnp.float32)
        right.append(jnp.concatenate([stacked, filler], axis=0).astype(jnp.bfloat16))
    for f in range(frames):
        acc = jnp.dot(taps_ref[...], right[f], preferred_element_type=jnp.float32)
        hidden = jax.nn.gelu(acc)
        high, rest = split(hidden, 2)
        first = jnp.dot(last_ref[...], high, preferred_element_type=jnp.float32)
        second = jnp.dot(last_ref[...], rest, preferred_element_type=jnp.float32)
        delta = first[0:3] + (first[8:11] + second[0:3])
        moved = line[f + 1][0:3] + delta
        for o in range(3):
            held[o, f : f + 1] = moved[o : o + 1]
    store = pltpu.make_async_copy(held, out_ref, sem)
    store.start()
    store.wait()


def refine(far, inputs, near, taps, last):
    frames, _, share = inputs.shape
    moved = pl.pallas_call(
        refine_kernel,
        out_shape=jax.ShapeDtypeStruct((3, frames, share), jnp.float32),
        in_specs=[pl.BlockSpec(memory_space=pltpu.VMEM)] * 5,
        out_specs=pl.BlockSpec(memory_space=pltpu.MemorySpace.HBM),
        scratch_shapes=[pltpu.VMEM((3, frames, share), jnp.float32), pltpu.SemaphoreType.DMA],
        compiler_params=pltpu.CompilerParams(vmem_limit_bytes=8 << 20),
        name="refine",
    )(far, inputs, near, taps, last)
    return jnp.transpose(moved, (1, 0, 2))


def local(features, query_frame, query_row, query_col, conv_weight, conv_bias, out_weight):
    frame_count, pix_count, chan = features.shape
    rows_here = pix_count // W
    tiles, groups = lax.axis_size("tile"), lax.axis_size("frame")
    plane, column, tower = mesh_groups()
    keep, send = pick(features, query_frame, query_row, query_col, rows_here)
    swap = [(i, i ^ 1) for i in range(tiles)]
    mine = keep + lax.ppermute(send, "tile", swap)
    wide, tall = len(plane[0]), len(column[0])
    rows = mine.shape[0] // wide
    got = lax.all_to_all(mine.reshape(wide, rows, chan), "frame", 0, 0, axis_index_groups=plane)
    piece = jnp.sum(got, axis=0)
    got = lax.all_to_all(jnp.broadcast_to(piece, (tall, rows, chan)), BOTH, 0, 0, axis_index_groups=column)
    piece = jnp.sum(got, axis=0)
    got = lax.all_to_all(jnp.broadcast_to(piece, (wide, rows, chan)), "frame", 0, 0, axis_index_groups=plane)
    own = got.reshape(wide * rows, chan)
    other = lax.ppermute(own, "tile", swap)
    parts = score(own, other, fetch(features, own), features, rows_here)
    members = 2 * tiles
    shape = parts.shape
    parts = lax.all_to_all(parts.reshape(members, *shape[2:]), BOTH, 0, 0, axis_index_groups=tower)
    inputs, far, near = merge(parts.reshape(shape), rows_here * tiles * W)
    near = lax.ppermute(near, "frame", [(i, i ^ 1) for i in range(groups)])
    far = lax.ppermute(far, "frame", far_pairs())
    taps, last_weight = prepare(conv_weight, conv_bias, out_weight)
    return refine(far, inputs, near, taps, last_weight)


def solution(mesh):
    in_specs = (P("frame", "tile", None), P(), P(), P(), P(), P(), P())
    out_specs = P("frame", None, "tile")
    return jax.shard_map(local, mesh=mesh, in_specs=in_specs, out_specs=out_specs, check_vma=False)
```
